256 devices in a mesh: ctx: 32 (over z, x), dp: 8 (over y, core).
Axes of the slice: x: 4, y: 4, z: 8, core: 2. Of those that a mesh axis runs over, the one named last changes fastest.
Arguments:
- queries: bfloat16 [4096, 4096], P('dp', 'ctx'), may hold values from -10 to 10
- corpus_keys: bfloat16 [32768, 1024], P('ctx'), may hold values from -4 to 4
- corpus_values: bfloat16 [32768, 1024], P('ctx'), may hold values from -6 to 6
- own_keys: bfloat16 [4096, 1024], P('dp'), may hold values from -6 to 6
- own_values: bfloat16 [4096, 1024], P('dp'), may hold values from -6 to 6
- conv_lengths: int32 [8, 4], P('dp'), may hold values from 1 to 256, 512 in all within a row
- cart_keys: bfloat16 [2048, 1024], P('dp'), may hold values from -4 to 4
- cart_values: bfloat16 [2048, 1024], P('dp'), may hold values from -6 to 6
Outputs:
- teacher_out: bfloat16 [4096, 4096], P('dp', 'ctx')
- grad_keys: float32 [2048, 1024], P('dp', 'ctx')
- grad_values: float32 [2048, 1024], P('dp', 'ctx')
The draws below stay inside these ranges and needn't reach their ends.
Inputs may be any that keep to these rules, and one draw needn't show every extreme that they name: `conv_lengths`: each row sums to 512; every row holds a conversation of 256 tokens.
All inputs are finite; a program needn't handle non-finite values.
Results may differ from the reference program's by a relative error of at most 0.007.
Values may be sent and summed in bfloat16 or wider, within the bound.
A program may use at most 128 MiB of HBM per device.

```python
import math
import jax
import jax.numpy as jnp
import numpy as np
from jax import lax

HEADS = 32
KV_HEADS = 8
HD = 128
CART = 2048
TOK_DEV = 512
CORP_DEV = 1024
CONVS = 4
LEN_MAX = 256
TOKENS = 4096
CORPUS = 32768
N_CTX = 32
N_DP = 8


def draw_queries(key, part):
    key = jax.random.fold_in(key, 23)
    values = jnp.clip(2.5 * jax.random.normal(key, (TOKENS, HEADS * HD), jnp.float32), -10.0, 10.0)
    return values.astype(jnp.bfloat16)


def draw_corpus_keys(key, part):
    key = jax.random.fold_in(key, 21)
    values = jnp.clip(jax.random.normal(key, (CORPUS, KV_HEADS * HD), jnp.float32), -4.0, 4.0)
    return values.astype(jnp.bfloat16)


def draw_cart_keys(key, part):
    key = jax.random.fold_in(key, 22)
    values = jnp.clip(jax.random.normal(key, (CART, KV_HEADS * HD), jnp.float32), -4.0, 4.0)
    return values.astype(jnp.bfloat16)


def level_of(stream_key, shape, split, low, largest):
    factor_of, own = 1.0, jax.random.fold_in(stream_key, 6)
    for axis_at, blocks in split:
        steps = jnp.exp(jax.random.uniform(jax.random.fold_in(own, axis_at), (blocks,), jnp.float32, low / len(split), largest / len(split)))
        factor_of = factor_of * jnp.repeat(steps, shape[axis_at] // blocks).reshape([-1 if axis == axis_at else 1 for axis in range(len(shape))])
    return factor_of


def length_profile(amount, total, reach, slope):
    weights = [(1 << 20) // math.isqrt(rank ** slope) + 1 for rank in range(2, amount + 1)]
    spare, holding = total - reach - (amount - 1), [1] * (amount - 1)
    while spare > 0:
        free = [i for i in range(amount - 1) if holding[i] < reach]
        mass, budget = sum([weights[i] for i in free]), spare
        for i in free:
            more = min(reach - holding[i], max(1, budget * weights[i] // mass), spare)
            holding[i] = holding[i] + more
            spare = spare - more
    return np.array([reach] + holding)


def uneven(stream_key, amount, total, bound, lean):
    if amount == 2:
        one = jax.random.randint(stream_key, (), max(1, total - bound), min(bound, total - 1) + 1)
        return jnp.stack([one, total - one])
    sizes = jnp.asarray(length_profile(amount, total, bound, lean), jnp.int32)
    pairs = (amount - 1) // 2
    donor, receiver = sizes[1:1 + 2 * pairs:2], sizes[2:2 + 2 * pairs:2]
    margin = jnp.minimum(donor - 1, bound - receiver)
    passed = jax.random.randint(jax.random.fold_in(stream_key, 1), (pairs,), 0, 1 << 20) % (margin + 1)
    sizes = sizes.at[1:1 + 2 * pairs:2].set(donor - passed).at[2:2 + 2 * pairs:2].set(receiver + passed)
    return sizes[jax.random.permutation(jax.random.fold_in(stream_key, 2), amount)]


def gaussian(stream_key, shape, width, bound, cuts=(), kind=jnp.bfloat16):
    drawn = jax.random.normal(stream_key, shape, jnp.float32) * width
    if len(cuts) > 0:
        drawn = level_of(stream_key, shape, cuts, -0.22, 0.18) * drawn
    return jnp.clip(drawn, min=-bound, max=bound).astype(kind)


def setup_inputs(seed: int = 0) -> dict:
    seeds = jax.random.split(jax.random.key(seed), 9)
    queries = draw_queries(jax.random.fold_in(seeds[8], 71), 0)
    corpus_keys = draw_corpus_keys(jax.random.fold_in(seeds[8], 71), 0)
    corpus_values = gaussian(seeds[2], (CORPUS, KV_HEADS * HD), 1.0, 6.0, ((0, 32),))
    own_keys = gaussian(seeds[3], (TOKENS, KV_HEADS * HD), 1.0, 6.0, ((0, 8),))
    own_values = gaussian(seeds[4], (TOKENS, KV_HEADS * HD), 1.0, 6.0, ((0, 8),))
    conv_lengths = jax.vmap(lambda own: uneven(own, CONVS, TOK_DEV, LEN_MAX, 2))(jax.random.split(seeds[5], N_DP)).reshape((N_DP, CONVS)).astype(jnp.int32)
    cart_keys = draw_cart_keys(jax.random.fold_in(seeds[8], 71), 0)
    cart_values = gaussian(seeds[7], (CART, KV_HEADS * HD), 1.0, 6.0, ((0, 8),))
    return dict(queries=queries, corpus_keys=corpus_keys, corpus_values=corpus_values, own_keys=own_keys, own_values=own_values, conv_lengths=conv_lengths, cart_keys=cart_keys, cart_values=cart_values)


def partial_block(query_rows, key_rows, value_rows, allowed):
    scores = jnp.dot(query_rows, key_rows.T, preferred_element_type=jnp.float32) * (1.0 / math.sqrt(HD))
    if allowed is not None:
        scores = jnp.where(allowed, scores, -jnp.inf)
    row_max = lax.optimization_barrier(jnp.max(scores, axis=1))
    exponent = jnp.exp(scores - row_max[:, None])
    weights = exponent.astype(jnp.bfloat16)
    row_total = lax.optimization_barrier(jnp.sum(exponent, axis=1))
    accumulated = jnp.dot(weights, value_rows, preferred_element_type=jnp.float32)
    return (accumulated, row_max, row_total, exponent, weights)

def conversation_mask(lengths, count):
    ends = jnp.cumsum(lengths, dtype=jnp.int32)
    position = jnp.arange(count, dtype=jnp.int32)
    conversation = lax.optimization_barrier(jnp.sum((position[:, None] >= ends[None, :]).astype(jnp.int32), axis=1))
    same = conversation[:, None] == conversation[None, :]
    return jnp.logical_and(same, position[None, :] <= position[:, None])

def merge_own(corpus_acc, corpus_total, corpus_peak, own_acc, own_max, own_total):
    joint = jnp.maximum(corpus_peak, own_max)
    far_scale = jnp.exp(corpus_peak - joint)
    near_scale = jnp.exp(own_max - joint)
    upper = far_scale[:, None] * corpus_acc + near_scale[:, None] * own_acc
    lower = far_scale * corpus_total + near_scale * own_total
    return upper / lower[:, None]

def student_terms(query_rows, key_rows, value_rows, allowed, teacher_rows, cart_count):
    accumulated, row_max, row_total, exponent, weights = partial_block(query_rows, key_rows, value_rows, allowed)
    student = accumulated / row_total[:, None]
    difference = student - teacher_rows.astype(jnp.float32)
    upstream = (difference / row_total[:, None]).astype(jnp.bfloat16)
    total_grad = -lax.optimization_barrier(jnp.sum(upstream.astype(jnp.float32) * student, axis=1))
    exponent_grad = jnp.dot(upstream, value_rows.T, preferred_element_type=jnp.float32) + total_grad[:, None]
    score_grad = (exponent * exponent_grad).astype(jnp.bfloat16)
    key_grad = jnp.dot(score_grad[:, :cart_count].T, query_rows, preferred_element_type=jnp.float32) * (1.0 / math.sqrt(HD))
    value_grad = jnp.dot(weights[:, :cart_count].T, upstream, preferred_element_type=jnp.float32)
    return (key_grad, value_grad)

def reference(queries, corpus_keys, corpus_values, own_keys, own_values, conv_lengths, cart_keys, cart_values):
    group_size = HEADS // KV_HEADS
    corpus_k = corpus_keys.reshape(N_CTX, CORP_DEV, KV_HEADS, HD)
    corpus_v = corpus_values.reshape(N_CTX, CORP_DEV, KV_HEADS, HD)
    cart_k = cart_keys.reshape(CART, KV_HEADS, HD)
    cart_v = cart_values.reshape(CART, KV_HEADS, HD)
    full_queries = queries.reshape(N_DP, TOK_DEV, HEADS, HD)
    own_k = own_keys.reshape(N_DP, TOK_DEV, KV_HEADS, HD)
    own_v = own_values.reshape(N_DP, TOK_DEV, KV_HEADS, HD)

    def one_block(inputs):
        block_queries, block_keys, block_values, lengths = inputs
        allowed = conversation_mask(lengths, TOK_DEV)
        full_allowed = jnp.concatenate([jnp.ones((TOK_DEV, CART), dtype=bool), allowed], axis=1)
        teacher_cols = []
        key_grads = [jnp.zeros((CART, HD), jnp.float32) for index in range(KV_HEADS)]
        value_grads = [jnp.zeros((CART, HD), jnp.float32) for index in range(KV_HEADS)]
        for head_index in range(HEADS):
            kv_index = head_index // group_size
            query_rows = block_queries[:, head_index]

            def per_block(key_rows, value_rows):
                return partial_block(query_rows, key_rows, value_rows, None)[:3]
            block_acc, block_max, block_total = jax.vmap(per_block)(corpus_k[:, :, kv_index], corpus_v[:, :, kv_index])
            corpus_peak = lax.optimization_barrier(jnp.max(block_max, axis=0))
            rescale = jnp.exp(block_max - corpus_peak[None, :])
            corpus_acc = lax.optimization_barrier(jnp.sum(rescale[:, :, None] * block_acc, axis=0))
            corpus_total = lax.optimization_barrier(jnp.sum(rescale * block_total, axis=0))
            own_key = block_keys[:, kv_index]
            own_value = block_values[:, kv_index]
            own_acc, own_max, own_total = partial_block(query_rows, own_key, own_value, allowed)[:3]
            teacher_rows = merge_own(corpus_acc, corpus_total, corpus_peak, own_acc, own_max, own_total).astype(jnp.bfloat16)
            teacher_cols.append(teacher_rows)
            joined_keys = jnp.concatenate([cart_k[:, kv_index], own_key], axis=0)
            joined_values = jnp.concatenate([cart_v[:, kv_index], own_value], axis=0)
            key_grad, value_grad = student_terms(query_rows, joined_keys, joined_values, full_allowed, teacher_rows, CART)
            key_grads[kv_index] = key_grads[kv_index] + key_grad
            value_grads[kv_index] = value_grads[kv_index] + value_grad
        return (jnp.concatenate(teacher_cols, axis=1), jnp.concatenate(key_grads, axis=1), jnp.concatenate(value_grads, axis=1))
    teacher_blocks, key_blocks, value_blocks = lax.map(one_block, (full_queries, own_k, own_v, conv_lengths))
    teacher_out = teacher_blocks.reshape(TOKENS, HEADS * HD)
    return (teacher_out, lax.optimization_barrier(jnp.sum(key_blocks, axis=0)), lax.optimization_barrier(jnp.sum(value_blocks, axis=0)))
```

```python
import math

import jax
import jax.numpy as jnp
from jax import lax
from jax.experimental import pallas as pl
from jax.experimental.pallas import tpu as pltpu
from jax.sharding import PartitionSpec as P

HEADS = 32
KV_HEADS = 8
HD = 128
TOK = 512
NX, NY, NZ = 4, 4, 8
GROUP = 4
SCALE = 1.0 / math.sqrt(HD)
LOG2 = SCALE * math.log2(math.e)
F32 = jnp.float32
BF16 = jnp.bfloat16
MESH = pl.DeviceIdType.MESH
HOPS = (0, 1, 7, 2, 6, 3, 5, 4)
CART_SLOTS = (8, 9)


def dot_nt(a, b):
    return lax.dot_general(a, b, (((1,), (1,)), ((), ())), preferred_element_type=F32)


def dot_tn(a, b):
    return lax.dot_general(a, b, (((0,), (0,)), ((), ())), preferred_element_type=F32)


def dot_nn(a, b):
    return jnp.dot(a, b, preferred_element_type=F32)


def step_kernel(
    q_hbm, ck, cv, ok, ov, lens, tk, tv, tout, gk_out, gv_out,
    kv, qv, qT, okv, acc, ml, own_acc, own_ml, cart_acc, w0,
    pa_s, pa_r, pm_s, pm_r, gc_s, gc_r, gvy_s, gvy_r, gvx_s, gvx_r, gkx_s, gkx_r, gky_s, gky_r,
    lsem, zs, zr, ys, yr, cs, cr, qs, qr, ps, pr, gcs, gcr, gas, gar, gbs, gbr,
):
    ctx = lax.axis_index("ctx")
    dp = lax.axis_index("dp")
    z, x = ctx // NX, lax.rem(ctx, NX)
    y, c = dp // 2, lax.rem(dp, 2)
    oc = 1 - c

    def dev(zz, xx, yy, cc):
        return (zz * NX + xx, yy * 2 + cc)

    def zof(t):
        return lax.rem(z + t, NZ)

    def xof(t):
        return lax.rem(x + t, NX)

    def yof(t):
        return lax.rem(y + t, NY)

    barrier = pltpu.get_barrier_semaphore()
    for t in range(1, NZ):
        pl.semaphore_signal(barrier, inc=1, device_id=dev(zof(t), x, y, c), device_id_type=MESH)
    for t in range(1, NX):
        pl.semaphore_signal(barrier, inc=1, device_id=dev(z, xof(t), y, c), device_id_type=MESH)
    for t in range(1, NY):
        pl.semaphore_signal(barrier, inc=1, device_id=dev(z, x, yof(t), c), device_id_type=MESH)
    pl.semaphore_signal(barrier, inc=1, device_id=dev(z, x, y, oc), device_id_type=MESH)

    def cols(zz):
        return pl.ds(pl.multiple_of(zz * HD, HD), HD)

    loads = [
        pltpu.make_async_copy(q_hbm, qv.at[0], lsem.at[0]),
        pltpu.make_async_copy(ok.at[:, cols(z)], okv.at[0], lsem.at[1]),
        pltpu.make_async_copy(ov.at[:, cols(z)], okv.at[1], lsem.at[2]),
    ]
    for j in range(2):
        loads.append(
            pltpu.make_async_copy(tk.at[j, :, cols(z)], kv.at[8 + j, y, c, 0], lsem.at[3 + 2 * j])
        )
        loads.append(
            pltpu.make_async_copy(tv.at[j, :, cols(z)], kv.at[8 + j, y, c, 1], lsem.at[4 + 2 * j])
        )
    loads.append(pltpu.make_async_copy(ck.at[:, :, :, cols(z)], kv.at[0, :, :, 0], lsem.at[7]))
    loads.append(pltpu.make_async_copy(cv.at[:, :, :, cols(z)], kv.at[0, :, :, 1], lsem.at[8]))
    for copy in loads:
        copy.start()

    for copy in loads[:3]:
        copy.wait()
    qT[0] = qv[0].T
    kpos = lax.broadcasted_iota(jnp.int32, (TOK, TOK), 0)
    qpos = lax.broadcasted_iota(jnp.int32, (TOK, TOK), 1)
    row = lax.broadcasted_iota(jnp.int32, (1, TOK), 1)
    begin = jnp.zeros((1, TOK), jnp.int32)
    end = jnp.int32(0)
    for i in range(4):
        end = end + lens[0, i]
        begin = jnp.where(row >= end, end, begin)
    allowed = jnp.logical_and(kpos >= begin, kpos <= qpos)
    s_own = jnp.where(allowed, dot_nn(okv[0], qT[0]), -jnp.inf)
    m_own = jnp.max(s_own, axis=0, keepdims=True)
    e_own = jnp.exp2((s_own - m_own) * LOG2)
    own_ml[0:1] = m_own
    own_ml[1:2] = jnp.sum(e_own, axis=0, keepdims=True)
    own_acc[...] = dot_tn(okv[1], e_own.astype(BF16))

    pl.semaphore_wait(barrier, NZ - 1 + NX - 1 + NY - 1 + 1)

    def q_copy(r):
        return pltpu.make_async_remote_copy(
            q_hbm, qv.at[r], qs.at[r], qr.at[r], dev(z, xof(NX - r), y, c), MESH
        )

    def z_copy(s, i):
        to = zof(NZ - HOPS[s])
        src = (ck, cv)[i].at[y, c, :, cols(to)]
        return pltpu.make_async_remote_copy(
            src, kv.at[s, y, c, i], zs.at[s, i], zr.at[s, i], dev(to, x, y, c), MESH
        )

    def y_copy(s, k, piece, to):
        ref = kv.at[s, yof(piece), c]
        return pltpu.make_async_remote_copy(
            ref, ref, ys.at[s, k], yr.at[s, k], dev(z, x, yof(to), c), MESH
        )

    def relay_up(s):
        return s % 2 == 0

    def y_send(s, k):
        if k < 2:
            return y_copy(s, k, 0, 1 if k == 0 else 3)
        return y_copy(s, 2, 3, 1) if relay_up(s) else y_copy(s, 2, 1, 3)

    def y_recv(s, k):
        return y_copy(s, k, (3, 1, 2)[k], 0)

    def c_copy(s, core):
        ref = kv.at[s, :, core]
        return pltpu.make_async_remote_copy(
            ref, ref, cs.at[s], cr.at[s], dev(z, x, y, oc), MESH
        )

    def stage1(s):
        if s < 8:
            z_copy(s, 0).wait_recv()
            z_copy(s, 1).wait_recv()
        y_send(s, 0).start()
        y_send(s, 1).start()

    def stage2(s):
        y_recv(s, 0 if relay_up(s) else 1).wait_recv()
        y_send(s, 2).start()

    def stage3(s):
        y_recv(s, 1 if relay_up(s) else 0).wait_recv()
        y_recv(s, 2).wait_recv()
        c_copy(s, c).start()

    def stage4(s):
        c_copy(s, oc).wait_recv()

    for s in (1, 2):
        for i in range(2):
            z_copy(s, i).start()
    for r in (1, 3, 2):
        q_copy(r).start()
    for s in range(3, 8):
        for i in range(2):
            z_copy(s, i).start()

    def unit(r, s0, n, first):
        keys = kv[s0 : s0 + n, :, :, 0].reshape(n * 1024, HD)
        values = kv[s0 : s0 + n, :, :, 1].reshape(n * 1024, HD)
        s = dot_nn(keys, qT[r])
        top = jnp.max(s, axis=0, keepdims=True)
        if not first:
            old = ml[r, 0:1]
            top = jnp.maximum(old, top)
            fade = jnp.exp2((old - top) * LOG2)
        e = jnp.exp2((s - top) * LOG2)
        total = jnp.sum(e, axis=0, keepdims=True)
        out = dot_tn(values, e.astype(BF16))
        if not first:
            total = total + fade * ml[r, 1:2]
            out = out + fade * acc[r]
        return r, top, total, out

    def keep(r, top, total, out):
        ml[r, 0:1] = top
        ml[r, 1:2] = total
        acc[r] = out

    def heads(todo, s0, n, first=False):
        done = [unit(r, s0, n, first) for r in todo]
        for item in done:
            keep(*item)

    loads[7].wait()
    loads[8].wait()
    heads((0,), 0, 1, True)
    stage1(1)
    for r in (1, 3, 2):
        q_copy(r).wait_recv()
        qT[r] = qv[r].T
    stage1(2)
    heads((1, 2, 3), 0, 1, True)
    stage2(1)
    stage2(2)
    stage1(3)
    stage3(1)
    stage1(4)
    stage3(2)
    stage4(1)
    stage4(2)

    def group(s0, n, actions):
        @pl.loop(0, 2)
        def _(i):
            heads((2 * i, 2 * i + 1), s0, n)
            for at in range(2):

                @pl.when(i == at)
                def _():
                    for act, s in actions[at]:
                        act(s)

    for copy in loads[3:7]:
        copy.wait()
    group(
        1, 2,
        [
            [(stage2, 3), (stage2, 4), (stage1, 8), (stage1, 9), (stage3, 3), (stage3, 4)],
            [(stage1, 5), (stage1, 6), (stage1, 7), (stage2, 8), (stage2, 9)],
        ],
    )
    stage4(3)
    stage4(4)
    group(
        3, 2,
        [
            [(stage3, 8), (stage3, 9), (stage2, 5), (stage2, 6), (stage2, 7)],
            [(stage3, 5), (stage3, 6), (stage3, 7)],
        ],
    )

    stage4(8)
    stage4(9)
    cart_keys = kv[8:10, :, :, 0].reshape(2048, HD)
    cart_values = kv[8:10, :, :, 1].reshape(2048, HD)
    s_cart = dot_nn(cart_keys, qT[0])
    m_cart = jnp.max(s_cart, axis=0, keepdims=True)
    e_cart = jnp.exp2((s_cart - m_cart) * LOG2)
    own_ml[2:3] = m_cart
    own_ml[3:4] = jnp.sum(e_cart, axis=0, keepdims=True)
    weights = e_cart.astype(BF16)
    w0[...] = weights.reshape(2, NY, 2, 128, TOK)
    cart_acc[...] = dot_tn(cart_values, weights)

    stage4(5)
    stage4(6)
    stage4(7)

    def p_copy(r, i):
        src, dst = ((pa_s, pa_r), (pm_s, pm_r))[i]
        return pltpu.make_async_remote_copy(
            src.at[r], dst.at[r], ps.at[r, i], pr.at[r, i], dev(z, xof(r), y, c), MESH
        )

    @pl.loop(0, 3)
    def _(i):
        r = 3 * (i // 2) + (2 - i) * (1 - i // 2)
        r, top, total, out = unit(r, 5, 3, False)
        pa_s[r] = out.astype(BF16)
        pm_s[r] = jnp.concatenate([top, total, jnp.zeros((6, TOK), F32)], axis=0)
        p_copy(r, 0).start()
        p_copy(r, 1).start()

    heads((0,), 5, 3)

    parts = [(ml[0, 0:1], ml[0, 1:2], acc[0])]
    for r in (2, 1, 3):
        p_copy(r, 0).wait_recv()
        p_copy(r, 1).wait_recv()
        parts.append((pm_r[r, 0:1], pm_r[r, 1:2], pa_r[r].astype(F32)))
    m_own, l_own = own_ml[0:1], own_ml[1:2]
    parts.append((m_own, l_own, own_acc[...]))
    joint = parts[0][0]
    for part in parts[1:]:
        joint = jnp.maximum(joint, part[0])
    lower = jnp.zeros((1, TOK), F32)
    upper = jnp.zeros((HD, TOK), F32)
    for top, total, out in parts:
        fade = jnp.exp2((top - joint) * LOG2)
        lower = lower + fade * total
        upper = upper + fade * out
    teacher = upper / lower
    tout[...] = teacher.T.astype(BF16)
    teacher = teacher.astype(BF16).astype(F32)

    m_cart, l_cart = own_ml[2:3], own_ml[3:4]
    top = jnp.maximum(m_own, m_cart)
    a_own = jnp.exp2((m_own - top) * LOG2)
    a_cart = jnp.exp2((m_cart - top) * LOG2)
    total = a_own * l_own + a_cart * l_cart
    student = (a_own * own_acc[...] + a_cart * cart_acc[...]) / total
    up = ((student - teacher) * (a_cart / total)).astype(BF16)
    up_sum = jnp.sum(up.astype(F32) * student, axis=0, keepdims=True)

    def half_weights(core):
        return w0[:, :, core].reshape(1024, TOK)

    def half_value_grad(core):
        return dot_nt(up, half_weights(core))

    def half_key_grad(core):
        values = kv[8:10, :, core, 1].reshape(1024, HD)
        score_grad = half_weights(core).astype(F32) * (dot_nn(values, up) - up_sum)
        return dot_nt(qT[0], score_grad.astype(BF16))

    def core_copy(i):
        return pltpu.make_async_remote_copy(
            gc_s.at[i], gc_r.at[i], gcs.at[i], gcr.at[i], dev(z, x, y, oc), MESH
        )

    gc_s[0] = half_value_grad(oc).astype(BF16)
    core_copy(0).start()
    gc_s[1] = half_key_grad(oc).astype(BF16)
    core_copy(1).start()
    value_grad = half_value_grad(c)

    def y_grad(i, src, dst, sems, semr, t):
        return pltpu.make_async_remote_copy(
            src.at[yof(t)], dst.at[t], sems.at[i, t], semr.at[i, t], dev(z, x, yof(t), c), MESH
        )

    def x_grad(i, src, dst, sems, semr, t):
        return pltpu.make_async_remote_copy(
            src.at[xof(t)], dst.at[t], sems.at[i, t], semr.at[i, t], dev(z, xof(t), y, c), MESH
        )

    core_copy(0).wait_recv()
    value_grad = value_grad + gc_r[0].astype(F32)
    for yy in range(NY):
        gvy_s[yy] = jnp.concatenate(
            [value_grad[:, 512 * j + 128 * yy : 512 * j + 128 * yy + 128] for j in range(2)], axis=1
        ).astype(BF16)
    for t in (2, 1, 3):
        y_grad(0, gvy_s, gvy_r, gas, gar, t).start()

    key_grad = half_key_grad(c)
    core_copy(1).wait_recv()
    key_grad = key_grad + gc_r[1].astype(F32)
    for xx in range(NX):
        gkx_s[xx] = key_grad[32 * xx : 32 * xx + 32].astype(BF16)
    for t in (2, 1, 3):
        x_grad(1, gkx_s, gkx_r, gas, gar, t).start()

    value_grad = gvy_s[y].astype(F32)
    for t in (2, 1, 3):
        y_grad(0, gvy_s, gvy_r, gas, gar, t).wait_recv()
        value_grad = value_grad + gvy_r[t].astype(F32)
    for xx in range(NX):
        gvx_s[xx] = value_grad[32 * xx : 32 * xx + 32].astype(BF16)
    for t in (2, 1, 3):
        x_grad(0, gvx_s, gvx_r, gbs, gbr, t).start()

    key_grad = gkx_s[x].astype(F32)
    for t in (2, 1, 3):
        x_grad(1, gkx_s, gkx_r, gas, gar, t).wait_recv()
        key_grad = key_grad + gkx_r[t].astype(F32)
    for yy in range(NY):
        gky_s[yy] = jnp.concatenate(
            [key_grad[:, 512 * j + 128 * yy : 512 * j + 128 * yy + 128] for j in range(2)], axis=1
        ).astype(BF16)
    for t in (2, 1, 3):
        y_grad(1, gky_s, gky_r, gbs, gbr, t).start()

    def flip(block):
        return jnp.concatenate([block, jnp.zeros((HD - 32, 256), F32)], axis=0).T[:, :32]

    value_grad = gvx_s[x].astype(F32)
    for t in (2, 1, 3):
        x_grad(0, gvx_s, gvx_r, gbs, gbr, t).wait_recv()
        value_grad = value_grad + gvx_r[t].astype(F32)
    gv_out[...] = flip(value_grad)

    key_grad = gky_s[y].astype(F32)
    for t in (2, 1, 3):
        y_grad(1, gky_s, gky_r, gbs, gbr, t).wait_recv()
        key_grad = key_grad + gky_r[t].astype(F32)
    gk_out[...] = flip(key_grad * SCALE)

    for r in range(1, NX):
        q_copy(r).wait_send()
        p_copy(r, 0).wait_send()
        p_copy(r, 1).wait_send()
    for s in range(1, 8):
        z_copy(s, 0).wait_send()
        z_copy(s, 1).wait_send()
    for s in range(1, 10):
        for k in range(3):
            y_send(s, k).wait_send()
        c_copy(s, c).wait_send()
    core_copy(0).wait_send()
    core_copy(1).wait_send()
    for t in range(1, 4):
        y_grad(0, gvy_s, gvy_r, gas, gar, t).wait_send()
        x_grad(1, gkx_s, gkx_r, gas, gar, t).wait_send()
        x_grad(0, gvx_s, gvx_r, gbs, gbr, t).wait_send()
        y_grad(1, gky_s, gky_r, gbs, gbr, t).wait_send()


def per_device(
    queries, corpus_keys, corpus_values, own_keys, own_values, conv_lengths, cart_keys, cart_values
):
    hbm = pl.BlockSpec(memory_space=pl.ANY)
    vmem = pl.BlockSpec(memory_space=pltpu.VMEM)
    smem = pl.BlockSpec(memory_space=pltpu.SMEM)
    dma = pltpu.SemaphoreType.DMA
    return pl.pallas_call(
        step_kernel,
        out_shape=(
            jax.ShapeDtypeStruct((TOK, HD), BF16),
            jax.ShapeDtypeStruct((256, 32), F32),
            jax.ShapeDtypeStruct((256, 32), F32),
        ),
        in_specs=[hbm, hbm, hbm, hbm, hbm, smem, hbm, hbm],
        out_specs=(vmem, vmem, vmem),
        scratch_shapes=[
            pltpu.VMEM((10, NY, 2, 2, 128, HD), BF16),
            pltpu.VMEM((GROUP, TOK, HD), BF16),
            pltpu.VMEM((GROUP, HD, TOK), BF16),
            pltpu.VMEM((2, TOK, HD), BF16),
            pltpu.VMEM((GROUP, HD, TOK), F32),
            pltpu.VMEM((GROUP, 8, TOK), F32),
            pltpu.VMEM((HD, TOK), F32),
            pltpu.VMEM((8, TOK), F32),
            pltpu.VMEM((HD, TOK), F32),
            pltpu.VMEM((2, NY, 2, 128, TOK), BF16),
            pltpu.VMEM((GROUP, HD, TOK), BF16),
            pltpu.VMEM((GROUP, HD, TOK), BF16),
            pltpu.VMEM((GROUP, 8, TOK), F32),
            pltpu.VMEM((GROUP, 8, TOK), F32),
            pltpu.VMEM((2, HD, 1024), BF16),
            pltpu.VMEM((2, HD, 1024), BF16),
            pltpu.VMEM((NY, HD, 256), BF16),
            pltpu.VMEM((NY, HD, 256), BF16),
            pltpu.VMEM((NX, 32, 256), BF16),
            pltpu.VMEM((NX, 32, 256), BF16),
            pltpu.VMEM((NX, 32, 1024), BF16),
            pltpu.VMEM((NX, 32, 1024), BF16),
            pltpu.VMEM((NY, 32, 256), BF16),
            pltpu.VMEM((NY, 32, 256), BF16),
            dma((9,)),
            dma((8, 2)), dma((8, 2)),
            dma((10, 3)), dma((10, 3)),
            dma((10,)), dma((10,)),
            dma((4,)), dma((4,)),
            dma((4, 2)), dma((4, 2)),
            dma((2,)), dma((2,)),
            dma((2, 4)), dma((2, 4)),
            dma((2, 4)), dma((2, 4)),
        ],
        compiler_params=pltpu.CompilerParams(
            collective_id=0, has_side_effects=True, vmem_limit_bytes=56 * 2**20
        ),
        name="cartridge_step",
    )(
        queries,
        corpus_keys.reshape(NY, 2, 128, KV_HEADS * HD),
        corpus_values.reshape(NY, 2, 128, KV_HEADS * HD),
        own_keys,
        own_values,
        conv_lengths,
        cart_keys.reshape(2, 128, KV_HEADS * HD),
        cart_values.reshape(2, 128, KV_HEADS * HD),
    )


def solution(mesh):
    placed = (
        P("dp", "ctx"),
        P("ctx", None),
        P("ctx", None),
        P("dp", None),
        P("dp", None),
        P("dp", None),
        P("dp", None),
        P("dp", None),
    )
    return jax.shard_map(
        per_device,
        mesh=mesh,
        in_specs=placed,
        out_specs=(P("dp", "ctx"), P("dp", "ctx"), P("dp", "ctx")),
        check_vma=False,
    )
```

```python
import math

import jax
import jax.numpy as jnp
from jax import lax
from jax.experimental import pallas as pl
from jax.experimental.pallas import tpu as pltpu
from jax.sharding import PartitionSpec as P

HEADS = 32
KV_HEADS = 8
HD = 128
TOK = 512
NX, NY, NZ = 4, 4, 8
GROUP = 4
SCALE = 1.0 / math.sqrt(HD)
LOG2 = SCALE * math.log2(math.e)
F32 = jnp.float32
BF16 = jnp.bfloat16
MESH = pl.DeviceIdType.MESH
HOPS = (0, 1, 7, 2, 6, 3, 5, 4)
CART_SLOTS = (8, 9)


def dot_nt(a, b):
    return lax.dot_general(a, b, (((1,), (1,)), ((), ())), preferred_element_type=F32)


def dot_tn(a, b):
    return lax.dot_general(a, b, (((0,), (0,)), ((), ())), preferred_element_type=F32)


def dot_nn(a, b):
    return jnp.dot(a, b, preferred_element_type=F32)


def step_kernel(
    q_hbm, ck, cv, ok, ov, lens, tk, tv, tout, gk_out, gv_out,
    kv, qv, qT, okv, acc, ml, own_acc, own_ml, cart_acc, w0,
    pa_s, pa_r, pm_s, pm_r, gc_s, gc_r, gvy_s, gvy_r, gvx_s, gvx_r, gkx_s, gkx_r, gky_s, gky_r,
    lsem, zs, zr, ys, yr, cs, cr, qs, qr, ps, pr, gcs, gcr, gas, gar, gbs, gbr,
):
    ctx = lax.axis_index("ctx")
    dp = lax.axis_index("dp")
    z, x = ctx // NX, lax.rem(ctx, NX)
    y, c = dp // 2, lax.rem(dp, 2)
    oc = 1 - c

    def dev(zz, xx, yy, cc):
        return (zz * NX + xx, yy * 2 + cc)

    def zof(t):
        return lax.rem(z + t, NZ)

    def xof(t):
        return lax.rem(x + t, NX)

    def yof(t):
        return lax.rem(y + t, NY)

    barrier = pltpu.get_barrier_semaphore()
    for t in range(1, NZ):
        pl.semaphore_signal(barrier, inc=1, device_id=dev(zof(t), x, y, c), device_id_type=MESH)
    for t in range(1, NX):
        pl.semaphore_signal(barrier, inc=1, device_id=dev(z, xof(t), y, c), device_id_type=MESH)
    for t in range(1, NY):
        pl.semaphore_signal(barrier, inc=1, device_id=dev(z, x, yof(t), c), device_id_type=MESH)
    pl.semaphore_signal(barrier, inc=1, device_id=dev(z, x, y, oc), device_id_type=MESH)

    def cols(zz):
        return pl.ds(pl.multiple_of(zz * HD, HD), HD)

    loads = [
        pltpu.make_async_copy(q_hbm, qv.at[0], lsem.at[0]),
        pltpu.make_async_copy(ok.at[:, cols(z)], okv.at[0], lsem.at[1]),
        pltpu.make_async_copy(ov.at[:, cols(z)], okv.at[1], lsem.at[2]),
    ]
    for j in range(2):
        loads.append(
            pltpu.make_async_copy(tk.at[j, :, cols(z)], kv.at[8 + j, y, c, 0], lsem.at[3 + 2 * j])
        )
        loads.append(
            pltpu.make_async_copy(tv.at[j, :, cols(z)], kv.at[8 + j, y, c, 1], lsem.at[4 + 2 * j])
        )
    loads.append(pltpu.make_async_copy(ck.at[:, :, :, cols(z)], kv.at[0, :, :, 0], lsem.at[7]))
    loads.append(pltpu.make_async_copy(cv.at[:, :, :, cols(z)], kv.at[0, :, :, 1], lsem.at[8]))
    for copy in loads:
        copy.start()

    for copy in loads[:3]:
        copy.wait()
    qT[0] = qv[0].T
    kpos = lax.broadcasted_iota(jnp.int32, (TOK, TOK), 0)
    qpos = lax.broadcasted_iota(jnp.int32, (TOK, TOK), 1)
    row = lax.broadcasted_iota(jnp.int32, (1, TOK), 1)
    begin = jnp.zeros((1, TOK), jnp.int32)
    end = jnp.int32(0)
    for i in range(4):
        end = end + lens[0, i]
        begin = jnp.where(row >= end, end, begin)
    allowed = jnp.logical_and(kpos >= begin, kpos <= qpos)
    s_own = jnp.where(allowed, dot_nn(okv[0], qT[0]), -jnp.inf)
    m_own = jnp.max(s_own, axis=0, keepdims=True)
    e_own = jnp.exp2((s_own - m_own) * LOG2)
    own_ml[0:1] = m_own
    own_ml[1:2] = jnp.sum(e_own, axis=0, keepdims=True)
    own_acc[...] = dot_tn(okv[1], e_own.astype(BF16))

    def unit(r, s0, n, first):
        if not first:
            top, total, out = ml[r, 0:1], ml[r, 1:2], acc[r]
        for at in range(s0, s0 + n):
            s = dot_nn(kv[at, :, :, 0].reshape(1024, HD), qT[r])
            new = jnp.max(s, axis=0, keepdims=True)
            if not first:
                new = jnp.maximum(top, new)
                fade = jnp.exp2((top - new) * LOG2)
            e = jnp.exp2((s - new) * LOG2)
            part = dot_tn(kv[at, :, :, 1].reshape(1024, HD), e.astype(BF16))
            weight = jnp.sum(e, axis=0, keepdims=True)
            if first:
                total, out = weight, part
            else:
                total, out = fade * total + weight, fade * out + part
            top, first = new, False
        return r, top, total, out

    def keep(r, top, total, out):
        ml[r, 0:1] = top
        ml[r, 1:2] = total
        acc[r] = out

    def heads(todo, s0, n, first=False):
        done = [unit(r, s0, n, first) for r in todo]
        for item in done:
            keep(*item)

    loads[7].wait()
    loads[8].wait()
    heads((0,), 0, 1, True)

    pl.semaphore_wait(barrier, NZ - 1 + NX - 1 + NY - 1 + 1)

    def q_copy(r):
        src, to = ((q_hbm, 3), (qv.at[3 - 2 * c], 1 + 2 * c), (q_hbm, 1))[r - 1]
        return pltpu.make_async_remote_copy(
            src, qv.at[r], qs.at[r], qr.at[r], dev(z, xof(to), y, c), MESH
        )

    def z_copy(s, i):
        to = zof(NZ - HOPS[s])
        rows = slice(None) if s <= 2 else y
        src = (ck, cv)[i].at[rows, c, :, cols(to)]
        return pltpu.make_async_remote_copy(
            src, kv.at[s, rows, c, i], zs.at[s, i], zr.at[s, i], dev(to, x, y, c), MESH
        )

    def y_copy(s, k, piece, to):
        ref = kv.at[s, yof(piece), c]
        return pltpu.make_async_remote_copy(
            ref, ref, ys.at[s, k], yr.at[s, k], dev(z, x, yof(to), c), MESH
        )

    def relay_up(s):
        return s % 2 == 0

    def y_send(s, k):
        if k < 2:
            return y_copy(s, k, 0, 1 if k == 0 else 3)
        return y_copy(s, 2, 3, 1) if relay_up(s) else y_copy(s, 2, 1, 3)

    def y_recv(s, k):
        return y_copy(s, k, (3, 1, 2)[k], 0)

    def c_copy(s, core):
        ref = kv.at[s, :, core]
        return pltpu.make_async_remote_copy(
            ref, ref, cs.at[s], cr.at[s], dev(z, x, y, oc), MESH
        )

    def stage1(s):
        if s < 8:
            z_copy(s, 0).wait_recv()
            z_copy(s, 1).wait_recv()
        y_send(s, 0).start()
        y_send(s, 1).start()

    def stage2(s):
        y_recv(s, 0 if relay_up(s) else 1).wait_recv()
        y_send(s, 2).start()

    def stage3(s):
        if s <= 2:
            z_copy(s, 0).wait_recv()
            z_copy(s, 1).wait_recv()
            c_copy(s, c).start()
            return
        y_recv(s, 1 if relay_up(s) else 0).wait_recv()
        y_recv(s, 2).wait_recv()
        c_copy(s, c).start()

    def stage4(s):
        c_copy(s, oc).wait_recv()

    def group(s0, n, actions):
        @pl.loop(0, 4)
        def _(i):
            heads((i,), s0, n)
            for at in range(4):

                @pl.when(i == at)
                def _():
                    for act, s in actions[at]:
                        act(s)

    def cartridge():
        cart_keys = kv[8:10, :, :, 0].reshape(2048, HD)
        cart_values = kv[8:10, :, :, 1].reshape(2048, HD)
        s_cart = dot_nn(cart_keys, qT[0])
        m_cart = jnp.max(s_cart, axis=0, keepdims=True)
        e_cart = jnp.exp2((s_cart - m_cart) * LOG2)
        own_ml[2:3] = m_cart
        own_ml[3:4] = jnp.sum(e_cart, axis=0, keepdims=True)
        weights = e_cart.astype(BF16)
        w0[...] = weights.reshape(2, NY, 2, 128, TOK)
        cart_acc[...] = dot_tn(cart_values, weights)

    def p_copy(i):
        src, dst = (pa_s, pa_r), (pm_s, pm_r)
        to = (1 + 2 * c, 3 - 2 * c, 1 + 2 * c)[i]
        return [
            pltpu.make_async_remote_copy(
                a.at[i], b.at[i], ps.at[i, j], pr.at[i, j], dev(z, xof(to), y, c), MESH
            )
            for j, (a, b) in enumerate((src, dst))
        ]

    def p_send(i, top, total, out):
        pa_s[i] = out.astype(BF16)
        pm_s[i] = jnp.concatenate([top, total, jnp.zeros((6, TOK), F32)], axis=0)
        for copy in p_copy(i):
            copy.start()

    def p_part(i):
        for copy in p_copy(i):
            copy.wait_recv()
        return pm_r[i, 0:1], pm_r[i, 1:2], pa_r[i].astype(F32)

    def merge(parts):
        joint = parts[0][0]
        for part in parts[1:]:
            joint = jnp.maximum(joint, part[0])
        lower = jnp.zeros((1, TOK), F32)
        upper = jnp.zeros((HD, TOK), F32)
        for top, total, out in parts:
            fade = jnp.exp2((top - joint) * LOG2)
            lower = lower + fade * total
            upper = upper + fade * out
        return joint, lower, upper

    for copy in loads[3:7]:
        copy.wait()
    for r in (1, 3):
        q_copy(r).start()
    for s in (1, 2, 3, 4):
        z_copy(s, 0).start()
        z_copy(s, 1).start()
    stage1(8)
    stage1(9)
    for r in (1, 3):
        q_copy(r).wait_recv()
    q_copy(2).start()
    for r in (1, 3):
        qT[r] = qv[r].T
    heads((1, 3), 0, 1, True)
    stage3(1)
    stage3(2)
    stage2(8)
    stage2(9)
    q_copy(2).wait_recv()
    qT[2] = qv[2].T
    heads((2,), 0, 1, True)
    for s in (5, 6, 7):
        z_copy(s, 0).start()
        z_copy(s, 1).start()
    stage1(3)
    stage1(4)
    stage4(1)
    stage4(2)
    group(
        1, 2,
        [
            [(stage3, 8), (stage3, 9)],
            [(stage2, 3), (stage2, 4)],
            [(stage4, 8), (stage4, 9)],
            [(stage3, 3), (stage3, 4), (stage1, 5), (stage1, 6)],
        ],
    )
    cartridge()
    stage1(7)
    stage4(3)
    stage4(4)
    group(
        3, 2,
        [
            [(stage2, 5), (stage2, 6)],
            [(stage2, 7)],
            [(stage3, 5), (stage3, 6), (stage3, 7)],
            [(stage4, 5), (stage4, 6), (stage4, 7)],
        ],
    )

    @pl.loop(0, 2)
    def _(i):
        _, top, total, out = unit(2 + i * (1 - 2 * c), 5, 3, False)
        for at in range(2):

            @pl.when(i == at)
            def _():
                p_send(at, top, total, out)

    part = unit(1 + 2 * c, 5, 3, False)[1:]
    p_send(2, *merge([part, p_part(0)]))
    heads((0,), 5, 3)

    m_own, l_own = own_ml[0:1], own_ml[1:2]
    parts = [(ml[0, 0:1], ml[0, 1:2], acc[0]), p_part(1), p_part(2), (m_own, l_own, own_acc[...])]
    joint, lower, upper = merge(parts)
    teacher = upper / lower
    tout[...] = teacher.T.astype(BF16)
    teacher = teacher.astype(BF16).astype(F32)

    m_cart, l_cart = own_ml[2:3], own_ml[3:4]
    top = jnp.maximum(m_own, m_cart)
    a_own = jnp.exp2((m_own - top) * LOG2)
    a_cart = jnp.exp2((m_cart - top) * LOG2)
    total = a_own * l_own + a_cart * l_cart
    student = (a_own * own_acc[...] + a_cart * cart_acc[...]) / total
    up = ((student - teacher) * (a_cart / total)).astype(BF16)
    up_sum = jnp.sum(up.astype(F32) * student, axis=0, keepdims=True)

    def half_weights(core):
        return w0[:, :, core].reshape(1024, TOK)

    def half_value_grad(core):
        return dot_nt(up, half_weights(core))

    def half_key_grad(core):
        values = kv[8:10, :, core, 1].reshape(1024, HD)
        score_grad = half_weights(core).astype(F32) * (dot_nn(values, up) - up_sum)
        return dot_nt(qT[0], score_grad.astype(BF16))

    def core_copy(i):
        return pltpu.make_async_remote_copy(
            gc_s.at[i], gc_r.at[i], gcs.at[i], gcr.at[i], dev(z, x, y, oc), MESH
        )

    gc_s[0] = half_value_grad(oc).astype(BF16)
    core_copy(0).start()
    gc_s[1] = half_key_grad(oc).astype(BF16)
    core_copy(1).start()
    value_grad = half_value_grad(c)

    def y_grad(i, src, dst, sems, semr, t):
        return pltpu.make_async_remote_copy(
            src.at[yof(t)], dst.at[t], sems.at[i, t], semr.at[i, t], dev(z, x, yof(t), c), MESH
        )

    def x_grad(i, src, dst, sems, semr, t):
        return pltpu.make_async_remote_copy(
            src.at[xof(t)], dst.at[t], sems.at[i, t], semr.at[i, t], dev(z, xof(t), y, c), MESH
        )

    core_copy(0).wait_recv()
    value_grad = value_grad + gc_r[0].astype(F32)
    for yy in range(NY):
        gvy_s[yy] = jnp.concatenate(
            [value_grad[:, 512 * j + 128 * yy : 512 * j + 128 * yy + 128] for j in range(2)], axis=1
        ).astype(BF16)
    for t in (2, 1, 3):
        y_grad(0, gvy_s, gvy_r, gas, gar, t).start()

    key_grad = half_key_grad(c)
    core_copy(1).wait_recv()
    key_grad = key_grad + gc_r[1].astype(F32)
    for xx in range(NX):
        gkx_s[xx] = key_grad[32 * xx : 32 * xx + 32].astype(BF16)
    for t in (2, 1, 3):
        x_grad(1, gkx_s, gkx_r, gas, gar, t).start()

    value_grad = gvy_s[y].astype(F32)
    for t in (2, 1, 3):
        y_grad(0, gvy_s, gvy_r, gas, gar, t).wait_recv()
        value_grad = value_grad + gvy_r[t].astype(F32)
    for xx in range(NX):
        gvx_s[xx] = value_grad[32 * xx : 32 * xx + 32].astype(BF16)
    for t in (2, 1, 3):
        x_grad(0, gvx_s, gvx_r, gbs, gbr, t).start()

    key_grad = gkx_s[x].astype(F32)
    for t in (2, 1, 3):
        x_grad(1, gkx_s, gkx_r, gas, gar, t).wait_recv()
        key_grad = key_grad + gkx_r[t].astype(F32)
    for yy in range(NY):
        gky_s[yy] = jnp.concatenate(
            [key_grad[:, 512 * j + 128 * yy : 512 * j + 128 * yy + 128] for j in range(2)], axis=1
        ).astype(BF16)
    for t in (2, 1, 3):
        y_grad(1, gky_s, gky_r, gbs, gbr, t).start()

    value_grad = gvx_s[x].astype(F32)
    for t in (2, 1, 3):
        x_grad(0, gvx_s, gvx_r, gbs, gbr, t).wait_recv()
        value_grad = value_grad + gvx_r[t].astype(F32)
    gv_out[...] = value_grad

    key_grad = gky_s[y].astype(F32)
    for t in (2, 1, 3):
        y_grad(1, gky_s, gky_r, gbs, gbr, t).wait_recv()
        key_grad = key_grad + gky_r[t].astype(F32)
    gk_out[...] = key_grad * SCALE

    for r in range(1, NX):
        q_copy(r).wait_send()
        for copy in p_copy(r - 1):
            copy.wait_send()
    for s in range(1, 8):
        z_copy(s, 0).wait_send()
        z_copy(s, 1).wait_send()
    for s in range(1, 10):
        if s > 2:
            for k in range(3):
                y_send(s, k).wait_send()
        c_copy(s, c).wait_send()
    core_copy(0).wait_send()
    core_copy(1).wait_send()
    for t in range(1, 4):
        y_grad(0, gvy_s, gvy_r, gas, gar, t).wait_send()
        x_grad(1, gkx_s, gkx_r, gas, gar, t).wait_send()
        x_grad(0, gvx_s, gvx_r, gbs, gbr, t).wait_send()
        y_grad(1, gky_s, gky_r, gbs, gbr, t).wait_send()


def hand_over(a, b, c, a_out, b_out, c_out):
    a_out[...] = a[...]
    b_out[...] = b[...]
    c_out[...] = c[...]


def per_device(
    queries, corpus_keys, corpus_values, own_keys, own_values, conv_lengths, cart_keys, cart_values
):
    hbm = pl.BlockSpec(memory_space=pl.ANY)
    vmem = pl.BlockSpec(memory_space=pltpu.VMEM)
    smem = pl.BlockSpec(memory_space=pltpu.SMEM)
    dma = pltpu.SemaphoreType.DMA
    shapes = (
        jax.ShapeDtypeStruct((TOK, HD), BF16),
        jax.ShapeDtypeStruct((32, 256), F32),
        jax.ShapeDtypeStruct((32, 256), F32),
    )
    made = pl.pallas_call(
        step_kernel,
        out_shape=shapes,
        in_specs=[hbm, hbm, hbm, hbm, hbm, smem, hbm, hbm],
        out_specs=(vmem, vmem, vmem),
        scratch_shapes=[
            pltpu.VMEM((10, NY, 2, 2, 128, HD), BF16),
            pltpu.VMEM((GROUP, TOK, HD), BF16),
            pltpu.VMEM((GROUP, HD, TOK), BF16),
            pltpu.VMEM((2, TOK, HD), BF16),
            pltpu.VMEM((GROUP, HD, TOK), F32),
            pltpu.VMEM((GROUP, 8, TOK), F32),
            pltpu.VMEM((HD, TOK), F32),
            pltpu.VMEM((8, TOK), F32),
            pltpu.VMEM((HD, TOK), F32),
            pltpu.VMEM((2, NY, 2, 128, TOK), BF16),
            pltpu.VMEM((3, HD, TOK), BF16),
            pltpu.VMEM((3, HD, TOK), BF16),
            pltpu.VMEM((3, 8, TOK), F32),
            pltpu.VMEM((3, 8, TOK), F32),
            pltpu.VMEM((2, HD, 1024), BF16),
            pltpu.VMEM((2, HD, 1024), BF16),
            pltpu.VMEM((NY, HD, 256), BF16),
            pltpu.VMEM((NY, HD, 256), BF16),
            pltpu.VMEM((NX, 32, 256), BF16),
            pltpu.VMEM((NX, 32, 256), BF16),
            pltpu.VMEM((NX, 32, 1024), BF16),
            pltpu.VMEM((NX, 32, 1024), BF16),
            pltpu.VMEM((NY, 32, 256), BF16),
            pltpu.VMEM((NY, 32, 256), BF16),
            dma((9,)),
            dma((8, 2)), dma((8, 2)),
            dma((10, 3)), dma((10, 3)),
            dma((10,)), dma((10,)),
            dma((4,)), dma((4,)),
            dma((3, 2)), dma((3, 2)),
            dma((2,)), dma((2,)),
            dma((2, 4)), dma((2, 4)),
            dma((2, 4)), dma((2, 4)),
        ],
        compiler_params=pltpu.CompilerParams(
            collective_id=0, has_side_effects=True, vmem_limit_bytes=56 * 2**20
        ),
        name="cartridge_step",
    )(
        queries,
        corpus_keys.reshape(NY, 2, 128, KV_HEADS * HD),
        corpus_values.reshape(NY, 2, 128, KV_HEADS * HD),
        own_keys,
        own_values,
        conv_lengths,
        cart_keys.reshape(2, 128, KV_HEADS * HD),
        cart_values.reshape(2, 128, KV_HEADS * HD),
    )
    teacher, key_grad, value_grad = pl.pallas_call(
        hand_over,
        out_shape=shapes,
        in_specs=[vmem] * 3,
        out_specs=(vmem,) * 3,
        name="hand_over",
    )(*made)
    return teacher, key_grad.T, value_grad.T


def solution(mesh):
    placed = (
        P("dp", "ctx"),
        P("ctx", None),
        P("ctx", None),
        P("dp", None),
        P("dp", None),
        P("dp", None),
        P("dp", None),
        P("dp", None),
    )
    return jax.shard_map(
        per_device,
        mesh=mesh,
        in_specs=placed,
        out_specs=(P("dp", "ctx"), P("dp", "ctx"), P("dp", "ctx")),
        check_vma=False,
    )
```

```python
import math

import jax
import jax.numpy as jnp
from jax import lax
from jax.experimental import pallas as pl
from jax.experimental.pallas import tpu as pltpu
from jax.sharding import PartitionSpec as P

HEADS = 32
KV_HEADS = 8
HD = 128
TOK = 512
NX, NY, NZ = 4, 4, 8
GROUP = 4
SCALE = 1.0 / math.sqrt(HD)
LOG2 = SCALE * math.log2(math.e)
F32 = jnp.float32
BF16 = jnp.bfloat16
MESH = pl.DeviceIdType.MESH
HOPS = (0, 1, 7, 6, 2, 5, 3, 4)
CART_SLOTS = (8, 9)


def dot_nt(a, b):
    return lax.dot_general(a, b, (((1,), (1,)), ((), ())), preferred_element_type=F32)


def dot_tn(a, b):
    return lax.dot_general(a, b, (((0,), (0,)), ((), ())), preferred_element_type=F32)


def dot_nn(a, b):
    return jnp.dot(a, b, preferred_element_type=F32)


def step_kernel(
    q_hbm, ck, cv, ok, ov, lens, tk, tv, tout, gk_out, gv_out,
    kv, qv, qT, okv, acc, ml, own_acc, own_ml, cart_acc, w0,
    sbuf, pa_s, pa_r, pm_s, pm_r, gc_s, gc_r, ya_s, ya_r, xa_s, xa_r, xb_s, xb_r, yb_s, yb_r,
    tbuf, gbuf, lsem, osem, zs, zr, ys, yr, cs, cr, qs, qr, ps, pr, gcs, gcr, yas, yar, xas, xar, xbs, xbr, ybs, ybr,
):
    ctx = lax.axis_index("ctx")
    dp = lax.axis_index("dp")
    z, x = ctx // NX, lax.rem(ctx, NX)
    y, c = dp // 2, lax.rem(dp, 2)
    oc = 1 - c

    def dev(zz, xx, yy, cc):
        return (zz * NX + xx, yy * 2 + cc)

    def zof(t):
        return lax.rem(z + t, NZ)

    def xof(t):
        return lax.rem(x + t, NX)

    def yof(t):
        return lax.rem(y + t, NY)

    stores = [
        pltpu.make_async_copy(src, dst, osem.at[i])
        for i, (src, dst) in enumerate(((tbuf, tout), (gbuf.at[0], gk_out), (gbuf.at[1], gv_out)))
    ]
    barrier = pltpu.get_barrier_semaphore()
    for t in range(1, NZ):
        pl.semaphore_signal(barrier, inc=1, device_id=dev(zof(t), x, y, c), device_id_type=MESH)
    for t in range(1, NX):
        pl.semaphore_signal(barrier, inc=1, device_id=dev(z, xof(t), y, c), device_id_type=MESH)
    for t in range(1, NY):
        pl.semaphore_signal(barrier, inc=1, device_id=dev(z, x, yof(t), c), device_id_type=MESH)
    pl.semaphore_signal(barrier, inc=1, device_id=dev(z, x, y, oc), device_id_type=MESH)

    def cols(zz):
        return pl.ds(pl.multiple_of(zz * HD, HD), HD)

    loads = [
        pltpu.make_async_copy(q_hbm, qv.at[0], lsem.at[0]),
        pltpu.make_async_copy(ok.at[:, cols(z)], okv.at[0], lsem.at[1]),
        pltpu.make_async_copy(ov.at[:, cols(z)], okv.at[1], lsem.at[2]),
    ]
    for j in range(2):
        loads.append(
            pltpu.make_async_copy(tk.at[j, :, cols(z)], kv.at[8 + j, y, c, 0], lsem.at[3 + 2 * j])
        )
        loads.append(
            pltpu.make_async_copy(tv.at[j, :, cols(z)], kv.at[8 + j, y, c, 1], lsem.at[4 + 2 * j])
        )
    loads.append(pltpu.make_async_copy(ck.at[:, :, :, cols(z)], kv.at[0, :, :, 0], lsem.at[7]))
    loads.append(pltpu.make_async_copy(cv.at[:, :, :, cols(z)], kv.at[0, :, :, 1], lsem.at[8]))
    for copy in loads:
        copy.start()

    pl.semaphore_wait(barrier, NZ - 1 + NX - 1 + NY - 1 + 1)


    def q_copy(r):
        return pltpu.make_async_remote_copy(
            q_hbm, qv.at[r], qs.at[r], qr.at[r], dev(z, xof(NX - r), y, c), MESH
        )

    def z_copy(s, i):
        to = zof(NZ - HOPS[s])
        rows = slice(None) if s == 1 else y
        src = (ck, cv)[i].at[rows, c, :, cols(to)]
        return pltpu.make_async_remote_copy(
            src, kv.at[s, rows, c, i], zs.at[s, i], zr.at[s, i], dev(to, x, y, c), MESH
        )

    def y_copy(s, k, piece):
        ref = kv.at[s, piece, c]
        return pltpu.make_async_remote_copy(
            ref, ref, ys.at[s, k], yr.at[s, k], dev(z, x, yof(k), c), MESH
        )

    def y_send(s, k):
        return y_copy(s, k, y)

    def y_recv(s, k):
        return y_copy(s, k, yof(NY - k))

    def c_copy(s, core):
        ref = kv.at[s, :, core]
        return pltpu.make_async_remote_copy(
            ref, ref, cs.at[s], cr.at[s], dev(z, x, y, oc), MESH
        )

    def z_wait(s):
        z_copy(s, 0).wait_recv()
        z_copy(s, 1).wait_recv()

    def stage1(s):
        if s < 8:
            z_wait(s)
        for k in (1, 3, 2):
            y_send(s, k).start()

    def stage3(s):
        if s == 1:
            z_wait(s)
        else:
            for k in (1, 3, 2):
                y_recv(s, k).wait_recv()
        c_copy(s, c).start()

    def stage4(s):
        c_copy(s, oc).wait_recv()

    def scores(slot, r):
        return dot_nn(kv[slot, :, :, 0].reshape(1024, HD), qT[r])

    def state(r):
        return ml[r, 0:1], ml[r, 1:2], acc[r]

    def keep(r, top, total, out):
        ml[r, 0:1] = top
        ml[r, 1:2] = total
        acc[r] = out

    def absorb(at, slot, before):
        s = sbuf[at]
        top = jnp.max(s, axis=0, keepdims=True)
        if before is not None:
            top = jnp.maximum(before[0], top)
        e = jnp.exp2((s - top) * LOG2)
        total = jnp.sum(e, axis=0, keepdims=True)
        out = dot_tn(kv[slot, :, :, 1].reshape(1024, HD), e.astype(BF16))
        if before is not None:
            fade = jnp.exp2((before[0] - top) * LOG2)
            total = fade * before[1] + total
            out = fade * before[2] + out
        return top, total, out

    def first_block(todo):
        for i, r in enumerate(todo):
            sbuf[i] = scores(0, r)
        for i, r in enumerate(todo):
            keep(r, *absorb(i, 0, None))

    def one_block(slot, half_way, at_end):
        sbuf[0] = scores(slot, 0)
        for r in range(4):
            if r < 3:
                sbuf[(r + 1) % 2] = scores(slot, r + 1)
            keep(r, *absorb(r % 2, slot, state(r)))
            for act, s in half_way if r == 1 else at_end if r == 3 else ():
                act(s)

    def group(s0, low, actions):
        sbuf[0] = scores(s0, low)

        @pl.loop(low, 4)
        def _(i):
            sbuf[1] = scores(s0 + 1, i)
            now = absorb(0, s0, state(i))
            sbuf[0] = scores(s0, jnp.minimum(i + 1, 3))
            keep(i, *absorb(1, s0 + 1, now))
            for at in range(low, 4):

                @pl.when(i == at)
                def _():
                    for act, s in actions[at - low]:
                        act(s)

    def own_block():
        for copy in loads[:3]:
            copy.wait()
        qT[0] = qv[0].T
        kpos = lax.broadcasted_iota(jnp.int32, (TOK, TOK), 0)
        qpos = lax.broadcasted_iota(jnp.int32, (TOK, TOK), 1)
        row = lax.broadcasted_iota(jnp.int32, (1, TOK), 1)
        begin = jnp.zeros((1, TOK), jnp.int32)
        end = jnp.int32(0)
        for i in range(4):
            end = end + lens[0, i]
            begin = jnp.where(row >= end, end, begin)
        allowed = jnp.logical_and(kpos >= begin, kpos <= qpos)
        s_own = jnp.where(allowed, dot_nn(okv[0], qT[0]), -jnp.inf)
        m_own = jnp.max(s_own, axis=0, keepdims=True)
        e_own = jnp.exp2((s_own - m_own) * LOG2)
        own_ml[0:1] = m_own
        own_ml[1:2] = jnp.sum(e_own, axis=0, keepdims=True)
        own_acc[...] = dot_tn(okv[1], e_own.astype(BF16))

    def cartridge():
        sbuf[0] = scores(8, 0)
        sbuf[1] = scores(9, 0)
        m_cart = jnp.maximum(
            jnp.max(sbuf[0], axis=0, keepdims=True), jnp.max(sbuf[1], axis=0, keepdims=True)
        )
        total = jnp.zeros((1, TOK), F32)
        out = jnp.zeros((HD, TOK), F32)
        for j in range(2):
            e_cart = jnp.exp2((sbuf[j] - m_cart) * LOG2)
            total = total + jnp.sum(e_cart, axis=0, keepdims=True)
            weights = e_cart.astype(BF16)
            w0[j] = weights.reshape(NY, 2, 128, TOK)
            out = out + dot_tn(kv[8 + j, :, :, 1].reshape(1024, HD), weights)
        own_ml[2:3] = m_cart
        own_ml[3:4] = total
        cart_acc[...] = out

    def p_copy(i):
        src, dst = (pa_s, pa_r), (pm_s, pm_r)
        to = (1 + 2 * c, 3 - 2 * c, 1 + 2 * c)[i]
        return [
            pltpu.make_async_remote_copy(
                a.at[i], b.at[i], ps.at[i, j], pr.at[i, j], dev(z, xof(to), y, c), MESH
            )
            for j, (a, b) in enumerate((src, dst))
        ]

    def p_send(i, top, total, out):
        pa_s[i] = out.astype(BF16)
        pm_s[i] = jnp.concatenate([top, total, jnp.zeros((6, TOK), F32)], axis=0)
        for copy in p_copy(i):
            copy.start()

    def p_part(i):
        for copy in p_copy(i):
            copy.wait_recv()
        return pm_r[i, 0:1], pm_r[i, 1:2], pa_r[i].astype(F32)

    def merge(parts):
        joint = parts[0][0]
        for part in parts[1:]:
            joint = jnp.maximum(joint, part[0])
        lower = jnp.zeros((1, TOK), F32)
        upper = jnp.zeros((HD, TOK), F32)
        for top, total, out in parts:
            fade = jnp.exp2((top - joint) * LOG2)
            lower = lower + fade * total
            upper = upper + fade * out
        return joint, lower, upper

    for copy in loads[3:7]:
        copy.wait()
    def z_start(*slots):
        for s in slots:
            z_copy(s, 0).start()
            z_copy(s, 1).start()

    def z_start(*slots):
        for s in slots:
            z_copy(s, 0).start()
            z_copy(s, 1).start()

    for r in (1, 3, 2):
        q_copy(r).start()
    z_start(1, 2, 3, 4, 5, 6, 7)
    stage1(8)
    stage1(9)
    own_block()
    loads[7].wait()
    loads[8].wait()
    first_block((0,))
    stage1(2)
    for r in (1, 3):
        q_copy(r).wait_recv()
        qT[r] = qv[r].T
    first_block((1, 3))
    stage1(3)
    stage3(1)
    q_copy(2).wait_recv()
    qT[2] = qv[2].T
    first_block((2,))
    stage3(8)
    stage3(9)
    stage1(4)
    stage1(5)
    stage4(1)
    one_block(1, [(stage3, 2)], [(stage1, 6), (stage4, 2)])
    one_block(2, [(stage3, 3)], [(stage1, 7), (stage4, 3)])
    one_block(3, [(stage3, 4)], [(stage3, 5), (stage4, 8), (stage4, 9), (stage4, 4), (stage4, 5)])
    group(4, 1, [[], [(stage3, 6)], [(stage3, 7), (stage4, 6)]])
    order = (2, 3 - 2 * c, 1 + 2 * c, 0)
    steps = (
        (0, 6), (1, 6), (2, 6), (0, 7), (1, 7), (3, 4), (3, 5), (2, 7), (3, 6), (3, 7),
    )
    sbuf[0] = scores(6, order[0])
    for k, (i, slot) in enumerate(steps):
        if k == 2:
            stage4(7)
        if k + 1 < len(steps):
            sbuf[(k + 1) % 2] = scores(steps[k + 1][1], order[steps[k + 1][0]])
        now = absorb(k % 2, slot, state(order[i]))
        if slot == 7 and i < 2:
            p_send(i, *now)
        elif slot == 7 and i == 2:
            p_send(2, *merge([now, p_part(0)]))
        else:
            keep(order[i], *now)
    cartridge()

    m_own, l_own = own_ml[0:1], own_ml[1:2]
    parts = [state(0), p_part(1), p_part(2), (m_own, l_own, own_acc[...])]
    joint, lower, upper = merge(parts)
    teacher = upper / lower
    tbuf[...] = teacher.T.astype(BF16)
    stores[0].start()
    teacher = teacher.astype(BF16).astype(F32)

    m_cart, l_cart = own_ml[2:3], own_ml[3:4]
    top = jnp.maximum(m_own, m_cart)
    a_own = jnp.exp2((m_own - top) * LOG2)
    a_cart = jnp.exp2((m_cart - top) * LOG2)
    total = a_own * l_own + a_cart * l_cart
    student = (a_own * own_acc[...] + a_cart * cart_acc[...]) / total
    up = ((student - teacher) * (a_cart / total)).astype(BF16)
    up_sum = jnp.sum(up.astype(F32) * student, axis=0, keepdims=True)

    def half_weights(core):
        return w0[:, :, core].reshape(1024, TOK)

    def half_value_grad(core):
        return dot_nt(up, half_weights(core))

    def half_key_grad(core):
        values = kv[8:10, :, core, 1].reshape(1024, HD)
        score_grad = half_weights(core).astype(F32) * (dot_nn(values, up) - up_sum)
        return dot_nt(qT[0], score_grad.astype(BF16))

    def core_copy(i):
        return pltpu.make_async_remote_copy(
            gc_s.at[i], gc_r.at[i], gcs.at[i], gcr.at[i], dev(z, x, y, oc), MESH
        )

    gc_s[0] = half_value_grad(oc).astype(BF16)
    core_copy(0).start()
    value_grad = half_value_grad(c)
    gc_s[1] = half_key_grad(oc).astype(BF16)
    core_copy(1).start()

    def ring(axis, i, src, dst, sems, semr, t):
        to, at = ((z, x, yof(t), c), yof(t)) if axis == "y" else ((z, xof(t), y, c), xof(t))
        return pltpu.make_async_remote_copy(
            src.at[i, at], dst.at[i, t], sems.at[i, t], semr.at[i, t], dev(*to), MESH
        )

    ya = ("y", ya_s, ya_r, yas, yar)
    xa = ("x", xa_s, xa_r, xas, xar)
    xb = ("x", xb_s, xb_r, xbs, xbr)
    yb = ("y", yb_s, yb_r, ybs, ybr)

    def ring_start(plan, i):
        for t in (2, 1, 3):
            ring(plan[0], i, *plan[1:], t).start()

    def ring_sum(plan, i):
        total = plan[1][i, y if plan[0] == "y" else x].astype(F32)
        for t in (2, 1, 3):
            ring(plan[0], i, *plan[1:], t).wait_recv()
            total = total + plan[2][i, t].astype(F32)
        return total

    def reduce_first(i, grad):
        grad = grad.astype(BF16)
        for yy in range(NY):
            ya_s[i, yy] = grad[:, 128 * yy : 128 * yy + 128]
        ring_start(ya, i)
        for xx in range(NX):
            xb_s[i, xx] = grad[32 * xx : 32 * xx + 32, 512:]
        ring_start(xb, i)

    def reduce_second(i):
        grad = ring_sum(ya, i).astype(BF16)
        for xx in range(NX):
            xa_s[i, xx] = grad[32 * xx : 32 * xx + 32]
        ring_start(xa, i)
        grad = ring_sum(xb, i).astype(BF16)
        for yy in range(NY):
            yb_s[i, yy] = grad[:, 128 * yy : 128 * yy + 128]
        ring_start(yb, i)

    core_copy(0).wait_recv()
    reduce_first(0, value_grad + gc_r[0].astype(F32))
    key_grad = half_key_grad(c)
    core_copy(1).wait_recv()
    reduce_first(1, (key_grad + gc_r[1].astype(F32)) * SCALE)
    reduce_second(0)
    reduce_second(1)
    for i in range(2):
        gbuf[1 - i, :, :128] = ring_sum(xa, i)
        gbuf[1 - i, :, 128:] = ring_sum(yb, i)
        stores[2 - i].start()

    for copy in stores:
        copy.wait()
    for r in range(1, NX):
        q_copy(r).wait_send()
        for copy in p_copy(r - 1):
            copy.wait_send()
    for s in range(1, 8):
        z_copy(s, 0).wait_send()
        z_copy(s, 1).wait_send()
    for s in range(1, 10):
        for k in range(1, NY if s > 1 else 1):
            y_send(s, k).wait_send()
        c_copy(s, c).wait_send()
    core_copy(0).wait_send()
    core_copy(1).wait_send()
    for t in range(1, 4):
        for i in range(2):
            for plan in (ya, xa, xb, yb):
                ring(plan[0], i, *plan[1:], t).wait_send()


def hand_over(a, b, c, a_out, b_out, c_out):
    a_out[...] = a[...]
    b_out[...] = b[...]
    c_out[...] = c[...]


def per_device(
    queries, corpus_keys, corpus_values, own_keys, own_values, conv_lengths, cart_keys, cart_values
):
    hbm = pl.BlockSpec(memory_space=pl.ANY)
    vmem = pl.BlockSpec(memory_space=pltpu.VMEM)
    smem = pl.BlockSpec(memory_space=pltpu.SMEM)
    dma = pltpu.SemaphoreType.DMA
    shapes = (
        jax.ShapeDtypeStruct((TOK, HD), BF16),
        jax.ShapeDtypeStruct((32, 256), F32),
        jax.ShapeDtypeStruct((32, 256), F32),
    )
    made = pl.pallas_call(
        step_kernel,
        out_shape=shapes,
        in_specs=[hbm, hbm, hbm, hbm, hbm, smem, hbm, hbm],
        out_specs=(hbm, hbm, hbm),
        scratch_shapes=[
            pltpu.VMEM((10, NY, 2, 2, 128, HD), BF16),
            pltpu.VMEM((GROUP, TOK, HD), BF16),
            pltpu.VMEM((GROUP, HD, TOK), BF16),
            pltpu.VMEM((2, TOK, HD), BF16),
            pltpu.VMEM((GROUP, HD, TOK), F32),
            pltpu.VMEM((GROUP, 8, TOK), F32),
            pltpu.VMEM((HD, TOK), F32),
            pltpu.VMEM((8, TOK), F32),
            pltpu.VMEM((HD, TOK), F32),
            pltpu.VMEM((2, NY, 2, 128, TOK), BF16),
            pltpu.VMEM((2, 1024, TOK), F32),
            pltpu.VMEM((3, HD, TOK), BF16),
            pltpu.VMEM((3, HD, TOK), BF16),
            pltpu.VMEM((3, 8, TOK), F32),
            pltpu.VMEM((3, 8, TOK), F32),
            pltpu.VMEM((2, HD, 1024), BF16),
            pltpu.VMEM((2, HD, 1024), BF16),
            pltpu.VMEM((2, NY, HD, 128), BF16),
            pltpu.VMEM((2, NY, HD, 128), BF16),
            pltpu.VMEM((2, NX, 32, 128), BF16),
            pltpu.VMEM((2, NX, 32, 128), BF16),
            pltpu.VMEM((2, NX, 32, 512), BF16),
            pltpu.VMEM((2, NX, 32, 512), BF16),
            pltpu.VMEM((2, NY, 32, 128), BF16),
            pltpu.VMEM((2, NY, 32, 128), BF16),
            pltpu.VMEM((TOK, HD), BF16),
            pltpu.VMEM((2, 32, 256), F32),
            dma((9,)),
            dma((3,)),
            dma((8, 2)), dma((8, 2)),
            dma((10, 4)), dma((10, 4)),
            dma((10,)), dma((10,)),
            dma((4,)), dma((4,)),
            dma((3, 2)), dma((3, 2)),
            dma((2,)), dma((2,)),
            dma((2, 4)), dma((2, 4)),
            dma((2, 4)), dma((2, 4)),
            dma((2, 4)), dma((2, 4)),
            dma((2, 4)), dma((2, 4)),
        ],
        compiler_params=pltpu.CompilerParams(
            collective_id=0, has_side_effects=True, vmem_limit_bytes=56 * 2**20
        ),
        name="cartridge_step",
    )(
        queries,
        corpus_keys.reshape(NY, 2, 128, KV_HEADS * HD),
        corpus_values.reshape(NY, 2, 128, KV_HEADS * HD),
        own_keys,
        own_values,
        conv_lengths,
        cart_keys.reshape(2, 128, KV_HEADS * HD),
        cart_values.reshape(2, 128, KV_HEADS * HD),
    )
    teacher, key_grad, value_grad = pl.pallas_call(
        hand_over,
        out_shape=shapes,
        in_specs=[vmem] * 3,
        out_specs=(vmem,) * 3,
        name="hand_over",
    )(*made)
    return teacher, key_grad.T, value_grad.T


def solution(mesh):
    placed = (
        P("dp", "ctx"),
        P("ctx", None),
        P("ctx", None),
        P("dp", None),
        P("dp", None),
        P("dp", None),
        P("dp", None),
        P("dp", None),
    )
    return jax.shard_map(
        per_device,
        mesh=mesh,
        in_specs=placed,
        out_specs=(P("dp", "ctx"), P("dp", "ctx"), P("dp", "ctx")),
        check_vma=False,
    )
```

```python
import math

import jax
import jax.numpy as jnp
from jax import lax
from jax.experimental import pallas as pl
from jax.experimental.pallas import tpu as pltpu
from jax.sharding import PartitionSpec as P

HEADS = 32
KV_HEADS = 8
HD = 128
TOK = 512
NX, NY, NZ = 4, 4, 8
GROUP = 4
SCALE = 1.0 / math.sqrt(HD)
LOG2 = SCALE * math.log2(math.e)
F32 = jnp.float32
BF16 = jnp.bfloat16
MESH = pl.DeviceIdType.MESH
HOPS = (0, 1, 7, 6, 2, 5, 3, 4)
CART_SLOTS = (8, 9)


def dot_nt(a, b):
    return lax.dot_general(a, b, (((1,), (1,)), ((), ())), preferred_element_type=F32)


def dot_tn(a, b):
    return lax.dot_general(a, b, (((0,), (0,)), ((), ())), preferred_element_type=F32)


def dot_nn(a, b):
    return jnp.dot(a, b, preferred_element_type=F32)


def step_kernel(
    q_hbm, ck, cv, ok, ov, lens, tk, tv, tout, gk_out, gv_out,
    kv, qv, qT, okv, acc, ml, own_acc, own_ml, cart_acc, w0,
    sbuf, pa_s, pa_r, pm_s, pm_r, gc_s, gc_r, ya_s, ya_r, xa_s, xa_r, xb_s, xb_r, yb_s, yb_r,
    tbuf, gbuf, lsem, osem, zs, zr, ys, yr, cs, cr, qs, qr, ps, pr, gcs, gcr, yas, yar, xas, xar, xbs, xbr, ybs, ybr,
):
    ctx = lax.axis_index("ctx")
    dp = lax.axis_index("dp")
    z, x = ctx // NX, lax.rem(ctx, NX)
    y, c = dp // 2, lax.rem(dp, 2)
    oc = 1 - c

    def dev(zz, xx, yy, cc):
        return (zz * NX + xx, yy * 2 + cc)

    def zof(t):
        return lax.rem(z + t, NZ)

    def xof(t):
        return lax.rem(x + t, NX)

    def yof(t):
        return lax.rem(y + t, NY)

    stores = [
        pltpu.make_async_copy(src, dst, osem.at[i])
        for i, (src, dst) in enumerate(((tbuf, tout), (gbuf.at[0], gk_out), (gbuf.at[1], gv_out)))
    ]
    barrier = pltpu.get_barrier_semaphore()
    for t in range(1, NZ):
        pl.semaphore_signal(barrier, inc=1, device_id=dev(zof(t), x, y, c), device_id_type=MESH)
    for t in range(1, NX):
        pl.semaphore_signal(barrier, inc=1, device_id=dev(z, xof(t), y, c), device_id_type=MESH)
    for t in range(1, NY):
        pl.semaphore_signal(barrier, inc=1, device_id=dev(z, x, yof(t), c), device_id_type=MESH)
    pl.semaphore_signal(barrier, inc=1, device_id=dev(z, x, y, oc), device_id_type=MESH)

    def cols(zz):
        return pl.ds(pl.multiple_of(zz * HD, HD), HD)

    loads = [
        pltpu.make_async_copy(q_hbm, qv.at[0], lsem.at[0]),
        pltpu.make_async_copy(ok.at[:, cols(z)], okv.at[0], lsem.at[1]),
        pltpu.make_async_copy(ov.at[:, cols(z)], okv.at[1], lsem.at[2]),
    ]
    for j in range(2):
        loads.append(
            pltpu.make_async_copy(tk.at[j, :, cols(z)], kv.at[8 + j, y, c, 0], lsem.at[3 + 2 * j])
        )
        loads.append(
            pltpu.make_async_copy(tv.at[j, :, cols(z)], kv.at[8 + j, y, c, 1], lsem.at[4 + 2 * j])
        )
    loads.append(pltpu.make_async_copy(ck.at[:, :, :, cols(z)], kv.at[0, :, :, 0], lsem.at[7]))
    loads.append(pltpu.make_async_copy(cv.at[:, :, :, cols(z)], kv.at[0, :, :, 1], lsem.at[8]))
    for copy in loads:
        copy.start()

    pl.semaphore_wait(barrier, NZ - 1 + NX - 1 + NY - 1 + 1)


    def q_copy(r):
        return pltpu.make_async_remote_copy(
            q_hbm, qv.at[r], qs.at[r], qr.at[r], dev(z, xof(NX - r), y, c), MESH
        )

    def z_copy(s, i):
        to = zof(NZ - HOPS[s])
        rows = slice(None) if s == 1 else y
        src = (ck, cv)[i].at[rows, c, :, cols(to)]
        return pltpu.make_async_remote_copy(
            src, kv.at[s, rows, c, i], zs.at[s, i], zr.at[s, i], dev(to, x, y, c), MESH
        )

    def y_copy(s, k, piece):
        ref = kv.at[s, piece, c]
        return pltpu.make_async_remote_copy(
            ref, ref, ys.at[s, k], yr.at[s, k], dev(z, x, yof(k), c), MESH
        )

    def y_send(s, k):
        return y_copy(s, k, y)

    def y_recv(s, k):
        return y_copy(s, k, yof(NY - k))

    def c_copy(s, core):
        ref = kv.at[s, :, core]
        return pltpu.make_async_remote_copy(
            ref, ref, cs.at[s], cr.at[s], dev(z, x, y, oc), MESH
        )

    def z_wait(s):
        z_copy(s, 0).wait_recv()
        z_copy(s, 1).wait_recv()

    def stage1(s):
        if s < 8:
            z_wait(s)
        for k in (1, 3, 2):
            y_send(s, k).start()

    def stage3(s):
        if s == 1:
            z_wait(s)
        else:
            for k in (1, 3, 2):
                y_recv(s, k).wait_recv()
        c_copy(s, c).start()

    def stage4(s):
        c_copy(s, oc).wait_recv()

    def scores(slot, r):
        return dot_nn(kv[slot, :, :, 0].reshape(1024, HD), qT[r])

    def state(r):
        return ml[r, 0:1], ml[r, 1:2], acc[r]

    def keep(r, top, total, out):
        ml[r, 0:1] = top
        ml[r, 1:2] = total
        acc[r] = out

    def absorb(at, slot, before):
        s = sbuf[at]
        top = jnp.max(s, axis=0, keepdims=True)
        if before is not None:
            top = jnp.maximum(before[0], top)
        e = jnp.exp2((s - top) * LOG2)
        total = jnp.sum(e, axis=0, keepdims=True)
        out = dot_tn(kv[slot, :, :, 1].reshape(1024, HD), e.astype(BF16))
        if before is not None:
            fade = jnp.exp2((before[0] - top) * LOG2)
            total = fade * before[1] + total
            out = fade * before[2] + out
        return top, total, out

    def first_block(todo):
        for i, r in enumerate(todo):
            sbuf[i] = scores(0, r)
        for i, r in enumerate(todo):
            keep(r, *absorb(i, 0, None))

    def others(due):
        sbuf[1] = scores(1, 1)
        for r in range(1, 4):
            if r < 3:
                sbuf[(r + 1) % 2] = scores(1, r + 1)
            keep(r, *absorb(r % 2, 1, state(r)))
        for act in due[0]:
            act[0](*act[1:])

        @pl.loop(0, 3)
        def _(g):
            slot = 2 * g + 2
            sbuf[0] = scores(slot, 2)

            @pl.loop(1, 4)
            def _(i):
                r = jnp.where(i == 3, 3, 3 - i)
                sbuf[1] = scores(slot + 1, r)
                now = absorb(0, slot, state(r))
                sbuf[0] = scores(slot, jnp.where(i == 1, 1, 3))
                now = absorb(1, slot + 1, now)
                keep(r, *now)

                @pl.when(g == 2)
                def _():
                    p_send(r, *now)

                for at, acts in due[1].items():

                    @pl.when(jnp.logical_and(g == at[0], i == at[1]))
                    def _():
                        for act in acts:
                            act[0](*act[1:])

            sbuf[0] = scores(slot - 1, 0)
            sbuf[1] = scores(slot, 0)
            now = absorb(0, slot - 1, state(0))
            keep(0, *absorb(1, slot, now))
            for at in range(2):

                @pl.when(g == at)
                def _():
                    stage4(2 * at + 4)
                    stage4(2 * at + 5)

        sbuf[0] = scores(7, 0)
        keep(0, *absorb(0, 7, state(0)))

    def own_block():
        for copy in loads[:3]:
            copy.wait()
        qT[0] = qv[0].T
        kpos = lax.broadcasted_iota(jnp.int32, (TOK, TOK), 0)
        qpos = lax.broadcasted_iota(jnp.int32, (TOK, TOK), 1)
        row = lax.broadcasted_iota(jnp.int32, (1, TOK), 1)
        begin = jnp.zeros((1, TOK), jnp.int32)
        end = jnp.int32(0)
        for i in range(4):
            end = end + lens[0, i]
            begin = jnp.where(row >= end, end, begin)
        allowed = jnp.logical_and(kpos >= begin, kpos <= qpos)
        s_own = jnp.where(allowed, dot_nn(okv[0], qT[0]), -jnp.inf)
        m_own = jnp.max(s_own, axis=0, keepdims=True)
        e_own = jnp.exp2((s_own - m_own) * LOG2)
        own_ml[0:1] = m_own
        own_ml[1:2] = jnp.sum(e_own, axis=0, keepdims=True)
        own_acc[...] = dot_tn(okv[1], e_own.astype(BF16))

    def cartridge():
        sbuf[0] = scores(8, 0)
        sbuf[1] = scores(9, 0)
        m_cart = jnp.maximum(
            jnp.max(sbuf[0], axis=0, keepdims=True), jnp.max(sbuf[1], axis=0, keepdims=True)
        )
        total = jnp.zeros((1, TOK), F32)
        out = jnp.zeros((HD, TOK), F32)
        for j in range(2):
            e_cart = jnp.exp2((sbuf[j] - m_cart) * LOG2)
            total = total + jnp.sum(e_cart, axis=0, keepdims=True)
            weights = e_cart.astype(BF16)
            w0[j] = weights.reshape(NY, 2, 128, TOK)
            out = out + dot_tn(kv[8 + j, :, :, 1].reshape(1024, HD), weights)
        own_ml[2:3] = m_cart
        own_ml[3:4] = total
        cart_acc[...] = out

    def p_copy(i):
        src, dst = (pa_s, pa_r), (pm_s, pm_r)
        return [
            pltpu.make_async_remote_copy(
                a.at[i - 1], b.at[i - 1], ps.at[i - 1, j], pr.at[i - 1, j], dev(z, xof(i), y, c), MESH
            )
            for j, (a, b) in enumerate((src, dst))
        ]

    def p_send(i, top, total, out):
        pa_s[i - 1] = out.astype(BF16)
        pm_s[i - 1] = jnp.concatenate(
            [row[:, HD * j : HD * j + HD] for row in (top, total) for j in range(4)], axis=0
        )
        for copy in p_copy(i):
            copy.start()

    def p_part(i):
        for copy in p_copy(i):
            copy.wait_recv()
        top, total = (
            jnp.concatenate([pm_r[i - 1, k + j : k + j + 1] for j in range(4)], axis=1)
            for k in (0, 4)
        )
        return top, total, pa_r[i - 1].astype(F32)

    def merge(parts):
        joint = parts[0][0]
        for part in parts[1:]:
            joint = jnp.maximum(joint, part[0])
        lower = jnp.zeros((1, TOK), F32)
        upper = jnp.zeros((HD, TOK), F32)
        for top, total, out in parts:
            fade = jnp.exp2((top - joint) * LOG2)
            lower = lower + fade * total
            upper = upper + fade * out
        return joint, lower, upper

    for copy in loads[3:7]:
        copy.wait()
    def z_start(*slots):
        for s in slots:
            z_copy(s, 0).start()
            z_copy(s, 1).start()

    def z_start(*slots):
        for s in slots:
            z_copy(s, 0).start()
            z_copy(s, 1).start()

    for r in (1, 3, 2):
        q_copy(r).start()
    z_start(1, 2, 3, 4)
    stage1(8)
    stage1(9)
    own_block()
    loads[7].wait()
    loads[8].wait()
    first_block((0,))
    z_start(5)
    for r in (1, 3):
        q_copy(r).wait_recv()
        qT[r] = qv[r].T
    first_block((1, 3))
    z_start(6, 7)
    stage1(2)
    q_copy(2).wait_recv()
    qT[2] = qv[2].T
    first_block((2,))
    stage3(1)
    stage1(3)
    stage3(8)
    stage3(9)
    stage4(1)
    others((
        [
            (stage1, 4), (stage1, 5), (stage3, 2), (stage4, 8), (stage4, 9), (cartridge,),
            (stage3, 3), (stage4, 2), (stage4, 3),
        ],
        {
            (0, 2): [(stage1, 6), (stage3, 4)],
            (0, 3): [
                (stage1, 7), (stage3, 5),
            ],
            (1, 2): [(stage3, 6)],
            (1, 3): [(stage3, 7)],
        },
    ))

    m_own, l_own = own_ml[0:1], own_ml[1:2]
    parts = [state(0), p_part(2), p_part(1), p_part(3), (m_own, l_own, own_acc[...])]
    joint, lower, upper = merge(parts)
    teacher = upper / lower
    tbuf[...] = teacher.T.astype(BF16)
    stores[0].start()
    teacher = teacher.astype(BF16).astype(F32)

    m_cart, l_cart = own_ml[2:3], own_ml[3:4]
    top = jnp.maximum(m_own, m_cart)
    a_own = jnp.exp2((m_own - top) * LOG2)
    a_cart = jnp.exp2((m_cart - top) * LOG2)
    total = a_own * l_own + a_cart * l_cart
    student = (a_own * own_acc[...] + a_cart * cart_acc[...]) / total
    up = ((student - teacher) * (a_cart / total)).astype(BF16)
    up_sum = jnp.sum(up.astype(F32) * student, axis=0, keepdims=True)

    def half_weights(core):
        return w0[:, :, core].reshape(1024, TOK)

    def half_value_grad(core):
        return dot_nt(up, half_weights(core))

    def half_key_grad(core):
        values = kv[8:10, :, core, 1].reshape(1024, HD)
        score_grad = half_weights(core).astype(F32) * (dot_nn(values, up) - up_sum)
        return dot_nt(qT[0], score_grad.astype(BF16))

    def core_copy(i):
        return pltpu.make_async_remote_copy(
            gc_s.at[i], gc_r.at[i], gcs.at[i], gcr.at[i], dev(z, x, y, oc), MESH
        )

    gc_s[0] = half_value_grad(oc).astype(BF16)
    core_copy(0).start()
    value_grad = half_value_grad(c)
    gc_s[1] = half_key_grad(oc).astype(BF16)
    core_copy(1).start()

    def ring(axis, i, src, dst, sems, semr, t):
        to, at = ((z, x, yof(t), c), yof(t)) if axis == "y" else ((z, xof(t), y, c), xof(t))
        return pltpu.make_async_remote_copy(
            src.at[i, at], dst.at[i, t], sems.at[i, t], semr.at[i, t], dev(*to), MESH
        )

    ya = ("y", ya_s, ya_r, yas, yar)
    xa = ("x", xa_s, xa_r, xas, xar)
    xb = ("x", xb_s, xb_r, xbs, xbr)
    yb = ("y", yb_s, yb_r, ybs, ybr)

    def ring_start(plan, i):
        for t in (2, 1, 3):
            ring(plan[0], i, *plan[1:], t).start()

    def ring_sum(plan, i):
        total = plan[1][i, y if plan[0] == "y" else x].astype(F32)
        for t in (2, 1, 3):
            ring(plan[0], i, *plan[1:], t).wait_recv()
            total = total + plan[2][i, t].astype(F32)
        return total

    def reduce_first(i, grad):
        grad = grad.astype(BF16)
        for yy in range(NY):
            ya_s[i, yy] = grad[:, 128 * yy : 128 * yy + 128]
        ring_start(ya, i)
        for xx in range(NX):
            xb_s[i, xx] = grad[32 * xx : 32 * xx + 32, 512:]
        ring_start(xb, i)

    def reduce_second(i):
        grad = ring_sum(ya, i).astype(BF16)
        for xx in range(NX):
            xa_s[i, xx] = grad[32 * xx : 32 * xx + 32]
        ring_start(xa, i)
        grad = ring_sum(xb, i).astype(BF16)
        for yy in range(NY):
            yb_s[i, yy] = grad[:, 128 * yy : 128 * yy + 128]
        ring_start(yb, i)

    core_copy(0).wait_recv()
    reduce_first(0, value_grad + gc_r[0].astype(F32))
    key_grad = half_key_grad(c)
    core_copy(1).wait_recv()
    reduce_first(1, (key_grad + gc_r[1].astype(F32)) * SCALE)
    reduce_second(0)
    reduce_second(1)
    for i in range(2):
        gbuf[1 - i, :, :128] = ring_sum(xa, i)
        gbuf[1 - i, :, 128:] = ring_sum(yb, i)
        stores[2 - i].start()

    for copy in stores:
        copy.wait()
    for r in range(1, NX):
        q_copy(r).wait_send()
        for copy in p_copy(r):
            copy.wait_send()
    for s in range(1, 8):
        z_copy(s, 0).wait_send()
        z_copy(s, 1).wait_send()
    for s in range(1, 10):
        for k in range(1, NY if s > 1 else 1):
            y_send(s, k).wait_send()
        c_copy(s, c).wait_send()
    core_copy(0).wait_send()
    core_copy(1).wait_send()
    for t in range(1, 4):
        for i in range(2):
            for plan in (ya, xa, xb, yb):
                ring(plan[0], i, *plan[1:], t).wait_send()


def hand_over(a, b, c, a_out, b_out, c_out):
    a_out[...] = a[...]
    b_out[...] = b[...]
    c_out[...] = c[...]


def per_device(
    queries, corpus_keys, corpus_values, own_keys, own_values, conv_lengths, cart_keys, cart_values
):
    hbm = pl.BlockSpec(memory_space=pl.ANY)
    vmem = pl.BlockSpec(memory_space=pltpu.VMEM)
    smem = pl.BlockSpec(memory_space=pltpu.SMEM)
    dma = pltpu.SemaphoreType.DMA
    shapes = (
        jax.ShapeDtypeStruct((TOK, HD), BF16),
        jax.ShapeDtypeStruct((32, 256), F32),
        jax.ShapeDtypeStruct((32, 256), F32),
    )
    made = pl.pallas_call(
        step_kernel,
        out_shape=shapes,
        in_specs=[hbm, hbm, hbm, hbm, hbm, smem, hbm, hbm],
        out_specs=(hbm, hbm, hbm),
        scratch_shapes=[
            pltpu.VMEM((10, NY, 2, 2, 128, HD), BF16),
            pltpu.VMEM((GROUP, TOK, HD), BF16),
            pltpu.VMEM((GROUP, HD, TOK), BF16),
            pltpu.VMEM((2, TOK, HD), BF16),
            pltpu.VMEM((GROUP, HD, TOK), F32),
            pltpu.VMEM((GROUP, 8, TOK), F32),
            pltpu.VMEM((HD, TOK), F32),
            pltpu.VMEM((8, TOK), F32),
            pltpu.VMEM((HD, TOK), F32),
            pltpu.VMEM((2, NY, 2, 128, TOK), BF16),
            pltpu.VMEM((2, 1024, TOK), F32),
            pltpu.VMEM((3, HD, TOK), BF16),
            pltpu.VMEM((3, HD, TOK), BF16),
            pltpu.VMEM((3, 8, HD), F32),
            pltpu.VMEM((3, 8, HD), F32),
            pltpu.VMEM((2, HD, 1024), BF16),
            pltpu.VMEM((2, HD, 1024), BF16),
            pltpu.VMEM((2, NY, HD, 128), BF16),
            pltpu.VMEM((2, NY, HD, 128), BF16),
            pltpu.VMEM((2, NX, 32, 128), BF16),
            pltpu.VMEM((2, NX, 32, 128), BF16),
            pltpu.VMEM((2, NX, 32, 512), BF16),
            pltpu.VMEM((2, NX, 32, 512), BF16),
            pltpu.VMEM((2, NY, 32, 128), BF16),
            pltpu.VMEM((2, NY, 32, 128), BF16),
            pltpu.VMEM((TOK, HD), BF16),
            pltpu.VMEM((2, 32, 256), F32),
            dma((9,)),
            dma((3,)),
            dma((8, 2)), dma((8, 2)),
            dma((10, 4)), dma((10, 4)),
            dma((10,)), dma((10,)),
            dma((4,)), dma((4,)),
            dma((3, 2)), dma((3, 2)),
            dma((2,)), dma((2,)),
            dma((2, 4)), dma((2, 4)),
            dma((2, 4)), dma((2, 4)),
            dma((2, 4)), dma((2, 4)),
            dma((2, 4)), dma((2, 4)),
        ],
        compiler_params=pltpu.CompilerParams(
            collective_id=0, has_side_effects=True, vmem_limit_bytes=56 * 2**20
        ),
        name="cartridge_step",
    )(
        queries,
        corpus_keys.reshape(NY, 2, 128, KV_HEADS * HD),
        corpus_values.reshape(NY, 2, 128, KV_HEADS * HD),
        own_keys,
        own_values,
        conv_lengths,
        cart_keys.reshape(2, 128, KV_HEADS * HD),
        cart_values.reshape(2, 128, KV_HEADS * HD),
    )
    teacher, key_grad, value_grad = pl.pallas_call(
        hand_over,
        out_shape=shapes,
        in_specs=[vmem] * 3,
        out_specs=(vmem,) * 3,
        name="hand_over",
    )(*made)
    return teacher, key_grad.T, value_grad.T


def solution(mesh):
    placed = (
        P("dp", "ctx"),
        P("ctx", None),
        P("ctx", None),
        P("dp", None),
        P("dp", None),
        P("dp", None),
        P("dp", None),
        P("dp", None),
    )
    return jax.shard_map(
        per_device,
        mesh=mesh,
        in_specs=placed,
        out_specs=(P("dp", "ctx"), P("dp", "ctx"), P("dp", "ctx")),
        check_vma=False,
    )
```

```python
import math

import jax
import jax.numpy as jnp
from jax import lax
from jax.experimental import pallas as pl
from jax.experimental.pallas import tpu as pltpu
from jax.sharding import PartitionSpec as P

HEADS = 32
KV_HEADS = 8
HD = 128
TOK = 512
NX, NY, NZ = 4, 4, 8
GROUP = 4
SCALE = 1.0 / math.sqrt(HD)
LOG2 = SCALE * math.log2(math.e)
F32 = jnp.float32
BF16 = jnp.bfloat16
MESH = pl.DeviceIdType.MESH
HOPS = (0, 1, 7, 6, 2, 5, 3, 4)
CART_SLOTS = (8, 9)


def dot_nt(a, b):
    return lax.dot_general(a, b, (((1,), (1,)), ((), ())), preferred_element_type=F32)


def dot_tn(a, b):
    return lax.dot_general(a, b, (((0,), (0,)), ((), ())), preferred_element_type=F32)


def dot_nn(a, b):
    return jnp.dot(a, b, preferred_element_type=F32)


def step_kernel(
    q_hbm, ck, cv, ok, ov, lens, tk, tv, tout, gk_out, gv_out,
    kv, qv, qT, okv, acc, ml, own_acc, own_ml, cart_acc, w0,
    sbuf, pa_s, pa_r, pm_s, pm_r, gc_s, gc_r, ya_s, ya_r, xa_s, xa_r, xb_s, xb_r, yb_s, yb_r,
    tbuf, gbuf, lsem, osem, zs, zr, ys, yr, cs, cr, qs, qr, ps, pr, gcs, gcr, yas, yar, xas, xar, xbs, xbr, ybs, ybr,
):
    ctx = lax.axis_index("ctx")
    dp = lax.axis_index("dp")
    z, x = ctx // NX, lax.rem(ctx, NX)
    y, c = dp // 2, lax.rem(dp, 2)
    oc = 1 - c

    def dev(zz, xx, yy, cc):
        return (zz * NX + xx, yy * 2 + cc)

    def zof(t):
        return lax.rem(z + t, NZ)

    def xof(t):
        return lax.rem(x + t, NX)

    def yof(t):
        return lax.rem(y + t, NY)

    stores = [
        pltpu.make_async_copy(src, dst, osem.at[i])
        for i, (src, dst) in enumerate(((tbuf, tout), (gbuf.at[0], gk_out), (gbuf.at[1], gv_out)))
    ]
    barrier = pltpu.get_barrier_semaphore()
    for t in range(1, NZ):
        pl.semaphore_signal(barrier, inc=1, device_id=dev(zof(t), x, y, c), device_id_type=MESH)
    for t in range(1, NX):
        pl.semaphore_signal(barrier, inc=1, device_id=dev(z, xof(t), y, c), device_id_type=MESH)
    for t in range(1, NY):
        pl.semaphore_signal(barrier, inc=1, device_id=dev(z, x, yof(t), c), device_id_type=MESH)
    pl.semaphore_signal(barrier, inc=1, device_id=dev(z, x, y, oc), device_id_type=MESH)

    def cols(zz):
        return pl.ds(pl.multiple_of(zz * HD, HD), HD)

    loads = [
        pltpu.make_async_copy(q_hbm, qv.at[0], lsem.at[0]),
        pltpu.make_async_copy(ok.at[:, cols(z)], okv.at[0], lsem.at[1]),
        pltpu.make_async_copy(ov.at[:, cols(z)], okv.at[1], lsem.at[2]),
    ]
    for j in range(2):
        loads.append(
            pltpu.make_async_copy(tk.at[j, :, cols(z)], kv.at[8 + j, y, c, 0], lsem.at[3 + 2 * j])
        )
        loads.append(
            pltpu.make_async_copy(tv.at[j, :, cols(z)], kv.at[8 + j, y, c, 1], lsem.at[4 + 2 * j])
        )
    loads.append(pltpu.make_async_copy(ck.at[:, :, :, cols(z)], kv.at[0, :, :, 0], lsem.at[7]))
    loads.append(pltpu.make_async_copy(cv.at[:, :, :, cols(z)], kv.at[0, :, :, 1], lsem.at[8]))
    for copy in loads:
        copy.start()

    pl.semaphore_wait(barrier, NZ - 1 + NX - 1 + NY - 1 + 1)


    def q_copy(r):
        return pltpu.make_async_remote_copy(
            q_hbm, qv.at[r], qs.at[r], qr.at[r], dev(z, xof(NX - r), y, c), MESH
        )

    def z_copy(s, i):
        to = zof(NZ - HOPS[s])
        rows = slice(None) if s == 1 else y
        src = (ck, cv)[i].at[rows, c, :, cols(to)]
        return pltpu.make_async_remote_copy(
            src, kv.at[s, rows, c, i], zs.at[s, i], zr.at[s, i], dev(to, x, y, c), MESH
        )

    def y_copy(s, k, piece):
        ref = kv.at[s, piece, c]
        return pltpu.make_async_remote_copy(
            ref, ref, ys.at[s, k], yr.at[s, k], dev(z, x, yof(k), c), MESH
        )

    def y_send(s, k):
        return y_copy(s, k, y)

    def y_recv(s, k):
        return y_copy(s, k, yof(NY - k))

    def c_copy(s, core):
        ref = kv.at[s, :, core]
        return pltpu.make_async_remote_copy(
            ref, ref, cs.at[s], cr.at[s], dev(z, x, y, oc), MESH
        )

    def z_wait(s):
        z_copy(s, 0).wait_recv()
        z_copy(s, 1).wait_recv()

    def stage1(s):
        if s < 8:
            z_wait(s)
        for k in (1, 3, 2):
            y_send(s, k).start()

    def stage3(s):
        if s == 1:
            z_wait(s)
        else:
            for k in (1, 3, 2):
                y_recv(s, k).wait_recv()
        c_copy(s, c).start()

    def stage4(s):
        c_copy(s, oc).wait_recv()

    def scores(slot, r):
        return dot_nn(kv[slot, :, :, 0].reshape(1024, HD), qT[r])

    def state(r):
        return ml[r, 0:1], ml[r, 1:2], acc[r]

    def keep(r, top, total, out):
        ml[r, 0:1] = top
        ml[r, 1:2] = total
        acc[r] = out

    def absorb(at, slot, before):
        s = sbuf[at]
        top = jnp.max(s, axis=0, keepdims=True)
        if before is not None:
            top = jnp.maximum(before[0], top)
        e = jnp.exp2((s - top) * LOG2)
        total = jnp.sum(e, axis=0, keepdims=True)
        out = dot_tn(kv[slot, :, :, 1].reshape(1024, HD), e.astype(BF16))
        if before is not None:
            fade = jnp.exp2((before[0] - top) * LOG2)
            total = fade * before[1] + total
            out = fade * before[2] + out
        return top, total, out

    def first_block(todo):
        for i, r in enumerate(todo):
            sbuf[i] = scores(0, r)
        for i, r in enumerate(todo):
            keep(r, *absorb(i, 0, None))

    def others(due):
        sbuf[1] = scores(1, 1)
        for r in range(1, 4):
            if r < 3:
                sbuf[(r + 1) % 2] = scores(1, r + 1)
            keep(r, *absorb(r % 2, 1, state(r)))
        for act in due[0]:
            act[0](*act[1:])

        @pl.loop(0, 3)
        def _(g):
            slot = 2 * g + 2
            sbuf[0] = scores(slot, 2)

            @pl.loop(1, 4)
            def _(i):
                r = jnp.where(i == 3, 3, 3 - i)
                sbuf[1] = scores(slot + 1, r)
                now = absorb(0, slot, state(r))
                sbuf[0] = scores(slot, jnp.where(i == 1, 1, 3))
                now = absorb(1, slot + 1, now)
                keep(r, *now)

                @pl.when(g == 2)
                def _():
                    p_send(r, *now)

                for at, acts in due[1].items():

                    @pl.when(jnp.logical_and(g == at[0], i == at[1]))
                    def _():
                        for act in acts:
                            act[0](*act[1:])

            sbuf[0] = scores(slot - 1, 0)
            sbuf[1] = scores(slot, 0)
            now = absorb(0, slot - 1, state(0))
            keep(0, *absorb(1, slot, now))
            for at in range(2):

                @pl.when(g == at)
                def _():
                    stage4(2 * at + 4)
                    stage4(2 * at + 5)

        sbuf[0] = scores(7, 0)
        keep(0, *absorb(0, 7, state(0)))

    def own_block():
        for copy in loads[:3]:
            copy.wait()
        qT[0] = qv[0].T
        kpos = lax.broadcasted_iota(jnp.int32, (TOK, TOK), 0)
        qpos = lax.broadcasted_iota(jnp.int32, (TOK, TOK), 1)
        row = lax.broadcasted_iota(jnp.int32, (1, TOK), 1)
        begin = jnp.zeros((1, TOK), jnp.int32)
        end = jnp.int32(0)
        for i in range(4):
            end = end + lens[0, i]
            begin = jnp.where(row >= end, end, begin)
        allowed = jnp.logical_and(kpos >= begin, kpos <= qpos)
        s_own = jnp.where(allowed, dot_nn(okv[0], qT[0]), -jnp.inf)
        m_own = jnp.max(s_own, axis=0, keepdims=True)
        e_own = jnp.exp2((s_own - m_own) * LOG2)
        own_ml[0:1] = m_own
        own_ml[1:2] = jnp.sum(e_own, axis=0, keepdims=True)
        own_acc[...] = dot_tn(okv[1], e_own.astype(BF16))

    def cartridge():
        sbuf[0] = scores(8, 0)
        sbuf[1] = scores(9, 0)
        m_cart = jnp.maximum(
            jnp.max(sbuf[0], axis=0, keepdims=True), jnp.max(sbuf[1], axis=0, keepdims=True)
        )
        total = jnp.zeros((1, TOK), F32)
        out = jnp.zeros((HD, TOK), F32)
        for j in range(2):
            e_cart = jnp.exp2((sbuf[j] - m_cart) * LOG2)
            total = total + jnp.sum(e_cart, axis=0, keepdims=True)
            weights = e_cart.astype(BF16)
            w0[j] = weights.reshape(NY, 2, 128, TOK)
            out = out + dot_tn(kv[8 + j, :, :, 1].reshape(1024, HD), weights)
        own_ml[2:3] = m_cart
        own_ml[3:4] = total
        cart_acc[...] = out

    def p_copy(i):
        src, dst = (pa_s, pa_r), (pm_s, pm_r)
        return [
            pltpu.make_async_remote_copy(
                a.at[i - 1], b.at[i - 1], ps.at[i - 1, j], pr.at[i - 1, j], dev(z, xof(i), y, c), MESH
            )
            for j, (a, b) in enumerate((src, dst))
        ]

    def p_send(i, top, total, out):
        pa_s[i - 1] = out.astype(BF16)
        pm_s[i - 1] = jnp.concatenate(
            [row[:, HD * j : HD * j + HD] for row in (top, total) for j in range(4)], axis=0
        )
        for copy in p_copy(i):
            copy.start()

    def p_part(i):
        for copy in p_copy(i):
            copy.wait_recv()
        top, total = (
            jnp.concatenate([pm_r[i - 1, k + j : k + j + 1] for j in range(4)], axis=1)
            for k in (0, 4)
        )
        return top, total, pa_r[i - 1].astype(F32)

    def merge(parts):
        joint = parts[0][0]
        for part in parts[1:]:
            joint = jnp.maximum(joint, part[0])
        lower = jnp.zeros((1, TOK), F32)
        upper = jnp.zeros((HD, TOK), F32)
        for top, total, out in parts:
            fade = jnp.exp2((top - joint) * LOG2)
            lower = lower + fade * total
            upper = upper + fade * out
        return joint, lower, upper

    for copy in loads[3:7]:
        copy.wait()
    def z_start(*slots):
        for s in slots:
            z_copy(s, 0).start()
            z_copy(s, 1).start()

    def z_start(*slots):
        for s in slots:
            z_copy(s, 0).start()
            z_copy(s, 1).start()

    for r in (1, 3, 2):
        q_copy(r).start()
    z_start(1, 2, 3, 4)
    stage1(8)
    stage1(9)
    own_block()
    loads[7].wait()
    loads[8].wait()
    first_block((0,))
    z_start(5)
    for r in (1, 3):
        q_copy(r).wait_recv()
        qT[r] = qv[r].T
    first_block((1, 3))
    z_start(6, 7)
    stage1(2)
    q_copy(2).wait_recv()
    qT[2] = qv[2].T
    first_block((2,))
    stage3(1)
    stage1(3)
    stage3(8)
    stage3(9)
    stage4(1)
    others((
        [
            (stage1, 4), (stage1, 5), (stage3, 2), (stage4, 8), (stage4, 9), (cartridge,),
            (stage3, 3), (stage4, 2), (stage4, 3),
        ],
        {
            (0, 2): [(stage1, 6), (stage3, 4)],
            (0, 3): [
                (stage1, 7), (stage3, 5),
            ],
            (1, 2): [(stage3, 6)],
            (1, 3): [(stage3, 7)],
        },
    ))

    m_own, l_own = own_ml[0:1], own_ml[1:2]
    m_cart, l_cart = own_ml[2:3], own_ml[3:4]
    top = jnp.maximum(m_own, m_cart)
    a_own = jnp.exp2((m_own - top) * LOG2)
    a_cart = jnp.exp2((m_cart - top) * LOG2)
    total = a_own * l_own + a_cart * l_cart
    cart_scale = a_cart / total
    student = (a_own * own_acc[...] + a_cart * cart_acc[...]) / total

    parts = [state(0), p_part(2), p_part(1), p_part(3), (m_own, l_own, own_acc[...])]
    joint, lower, upper = merge(parts)
    teacher = upper / lower
    teacher = teacher.astype(BF16).astype(F32)

    up = ((student - teacher) * cart_scale).astype(BF16)
    up_sum = jnp.sum(up.astype(F32) * student, axis=0, keepdims=True)

    def half_weights(core):
        return w0[:, :, core].reshape(1024, TOK)

    def half_value_grad(core):
        return dot_nt(up, half_weights(core))

    def half_key_grad(core):
        values = kv[8:10, :, core, 1].reshape(1024, HD)
        score_grad = half_weights(core).astype(F32) * (dot_nn(values, up) - up_sum)
        return dot_nt(qT[0], score_grad.astype(BF16))

    def core_copy(i):
        return pltpu.make_async_remote_copy(
            gc_s.at[i], gc_r.at[i], gcs.at[i], gcr.at[i], dev(z, x, y, oc), MESH
        )

    gc_s[0] = half_value_grad(oc).astype(BF16)
    core_copy(0).start()
    value_grad = half_value_grad(c)
    gc_s[1] = half_key_grad(oc).astype(BF16)
    core_copy(1).start()

    def ring(axis, i, src, dst, sems, semr, t):
        to, at = ((z, x, yof(t), c), yof(t)) if axis == "y" else ((z, xof(t), y, c), xof(t))
        return pltpu.make_async_remote_copy(
            src.at[i, at], dst.at[i, t], sems.at[i, t], semr.at[i, t], dev(*to), MESH
        )

    ya = ("y", ya_s, ya_r, yas, yar)
    xa = ("x", xa_s, xa_r, xas, xar)
    xb = ("x", xb_s, xb_r, xbs, xbr)
    yb = ("y", yb_s, yb_r, ybs, ybr)

    def ring_start(plan, i):
        for t in (2, 1, 3):
            ring(plan[0], i, *plan[1:], t).start()

    def ring_sum(plan, i):
        total = plan[1][i, y if plan[0] == "y" else x].astype(F32)
        for t in (2, 1, 3):
            ring(plan[0], i, *plan[1:], t).wait_recv()
            total = total + plan[2][i, t].astype(F32)
        return total

    def reduce_first(i, grad):
        grad = grad.astype(BF16)
        for yy in range(NY):
            ya_s[i, yy] = grad[:, 128 * yy : 128 * yy + 128]
        ring_start(ya, i)
        for xx in range(NX):
            xb_s[i, xx] = grad[32 * xx : 32 * xx + 32, 512:]
        ring_start(xb, i)

    def reduce_second(i):
        grad = ring_sum(ya, i).astype(BF16)
        for xx in range(NX):
            xa_s[i, xx] = grad[32 * xx : 32 * xx + 32]
        ring_start(xa, i)
        grad = ring_sum(xb, i).astype(BF16)
        for yy in range(NY):
            yb_s[i, yy] = grad[:, 128 * yy : 128 * yy + 128]
        ring_start(yb, i)

    tbuf[...] = teacher.T.astype(BF16)
    stores[0].start()
    core_copy(0).wait_recv()
    reduce_first(0, value_grad + gc_r[0].astype(F32))
    key_grad = half_key_grad(c)
    core_copy(1).wait_recv()
    reduce_first(1, (key_grad + gc_r[1].astype(F32)) * SCALE)
    reduce_second(0)
    reduce_second(1)
    for i in range(2):
        gbuf[1 - i, :, :128] = ring_sum(xa, i)
        gbuf[1 - i, :, 128:] = ring_sum(yb, i)
        stores[2 - i].start()

    for copy in stores:
        copy.wait()
    for r in range(1, NX):
        q_copy(r).wait_send()
        for copy in p_copy(r):
            copy.wait_send()
    for s in range(1, 8):
        z_copy(s, 0).wait_send()
        z_copy(s, 1).wait_send()
    for s in range(1, 10):
        for k in range(1, NY if s > 1 else 1):
            y_send(s, k).wait_send()
        c_copy(s, c).wait_send()
    core_copy(0).wait_send()
    core_copy(1).wait_send()
    for t in range(1, 4):
        for i in range(2):
            for plan in (ya, xa, xb, yb):
                ring(plan[0], i, *plan[1:], t).wait_send()


def hand_over(a, b, c, a_out, b_out, c_out):
    a_out[...] = a[...]
    b_out[...] = b[...]
    c_out[...] = c[...]


def per_device(
    queries, corpus_keys, corpus_values, own_keys, own_values, conv_lengths, cart_keys, cart_values
):
    hbm = pl.BlockSpec(memory_space=pl.ANY)
    vmem = pl.BlockSpec(memory_space=pltpu.VMEM)
    smem = pl.BlockSpec(memory_space=pltpu.SMEM)
    dma = pltpu.SemaphoreType.DMA
    shapes = (
        jax.ShapeDtypeStruct((TOK, HD), BF16),
        jax.ShapeDtypeStruct((32, 256), F32),
        jax.ShapeDtypeStruct((32, 256), F32),
    )
    made = pl.pallas_call(
        step_kernel,
        out_shape=shapes,
        in_specs=[hbm, hbm, hbm, hbm, hbm, smem, hbm, hbm],
        out_specs=(hbm, hbm, hbm),
        scratch_shapes=[
            pltpu.VMEM((10, NY, 2, 2, 128, HD), BF16),
            pltpu.VMEM((GROUP, TOK, HD), BF16),
            pltpu.VMEM((GROUP, HD, TOK), BF16),
            pltpu.VMEM((2, TOK, HD), BF16),
            pltpu.VMEM((GROUP, HD, TOK), F32),
            pltpu.VMEM((GROUP, 8, TOK), F32),
            pltpu.VMEM((HD, TOK), F32),
            pltpu.VMEM((8, TOK), F32),
            pltpu.VMEM((HD, TOK), F32),
            pltpu.VMEM((2, NY, 2, 128, TOK), BF16),
            pltpu.VMEM((2, 1024, TOK), F32),
            pltpu.VMEM((3, HD, TOK), BF16),
            pltpu.VMEM((3, HD, TOK), BF16),
            pltpu.VMEM((3, 8, HD), F32),
            pltpu.VMEM((3, 8, HD), F32),
            pltpu.VMEM((2, HD, 1024), BF16),
            pltpu.VMEM((2, HD, 1024), BF16),
            pltpu.VMEM((2, NY, HD, 128), BF16),
            pltpu.VMEM((2, NY, HD, 128), BF16),
            pltpu.VMEM((2, NX, 32, 128), BF16),
            pltpu.VMEM((2, NX, 32, 128), BF16),
            pltpu.VMEM((2, NX, 32, 512), BF16),
            pltpu.VMEM((2, NX, 32, 512), BF16),
            pltpu.VMEM((2, NY, 32, 128), BF16),
            pltpu.VMEM((2, NY, 32, 128), BF16),
            pltpu.VMEM((TOK, HD), BF16),
            pltpu.VMEM((2, 32, 256), F32),
            dma((9,)),
            dma((3,)),
            dma((8, 2)), dma((8, 2)),
            dma((10, 4)), dma((10, 4)),
            dma((10,)), dma((10,)),
            dma((4,)), dma((4,)),
            dma((3, 2)), dma((3, 2)),
            dma((2,)), dma((2,)),
            dma((2, 4)), dma((2, 4)),
            dma((2, 4)), dma((2, 4)),
            dma((2, 4)), dma((2, 4)),
            dma((2, 4)), dma((2, 4)),
        ],
        compiler_params=pltpu.CompilerParams(
            collective_id=0, has_side_effects=True, vmem_limit_bytes=56 * 2**20
        ),
        name="cartridge_step",
    )(
        queries,
        corpus_keys.reshape(NY, 2, 128, KV_HEADS * HD),
        corpus_values.reshape(NY, 2, 128, KV_HEADS * HD),
        own_keys,
        own_values,
        conv_lengths,
        cart_keys.reshape(2, 128, KV_HEADS * HD),
        cart_values.reshape(2, 128, KV_HEADS * HD),
    )
    teacher, key_grad, value_grad = pl.pallas_call(
        hand_over,
        out_shape=shapes,
        in_specs=[vmem] * 3,
        out_specs=(vmem,) * 3,
        name="hand_over",
    )(*made)
    return teacher, key_grad.T, value_grad.T


def solution(mesh):
    placed = (
        P("dp", "ctx"),
        P("ctx", None),
        P("ctx", None),
        P("dp", None),
        P("dp", None),
        P("dp", None),
        P("dp", None),
        P("dp", None),
    )
    return jax.shard_map(
        per_device,
        mesh=mesh,
        in_specs=placed,
        out_specs=(P("dp", "ctx"), P("dp", "ctx"), P("dp", "ctx")),
        check_vma=False,
    )
```
